256 devices in a mesh: section: 16 (over x_lo, y, core), tensor: 16 (over x_hi, z).
Axes of the slice: x: 4 (x_hi: 2, x_lo: 2; x = x_hi * 2 + x_lo), y: 4, z: 8, core: 2. Of those that a mesh axis runs over, the one named last changes fastest.
Arguments:
- queries: bfloat16 [1024, 128, 128], P('section', 'tensor'), may hold values from -48 to 48
- kv_pool: bfloat16 [8, 64, 128, 256], P(None, 'section'), may hold values from -16 to 16
- block_table: int32 [1024, 4], P('section'), may hold values from 0 to 3
- cached_lengths: int32 [1024], P('section'), may hold values from 2 to 512
- arrivals: bfloat16 [8, 128, 128, 256], P(None, 'section'), may hold values from -6 to 6
- arrival_section: int32 [128], P('section'), may hold values from 0 to 15, as said below
- arrival_row: int32 [128], P('section'), may hold values from 0 to 63
- out_weight: bfloat16 [16384, 12288], P('tensor', 'section'), may hold values from -0.046875 to 0.046875
- residual: bfloat16 [1024, 12288], P('tensor', 'section'), may hold values from -40 to 40
- norm_gain: bfloat16 [12288], P('section'), may hold values from 0.099609375 to 1.8984375
- gate_weight: bfloat16 [12288, 26624], P('section', 'tensor'), may hold values from -0.0546875 to 0.0546875
- up_weight: bfloat16 [12288, 26624], P('section', 'tensor'), may hold values from -0.0546875 to 0.0546875
Outputs:
- attn_proj: float32 [1024, 12288], P('tensor', 'section')
- hidden: float32 [1024, 26624], P('section', 'tensor')
The draws below stay inside these ranges and needn't reach their ends.
Inputs may be any that keep to these rules, and one draw needn't show every extreme that they name: `arrival_section`: each section's 8 entries name one destination section at most 2 times; in every draw some destination section is named exactly 2 times by the entries of every section.
All inputs are finite; a program needn't handle non-finite values.
Results may differ from the reference program's by a relative error of at most 0.02.
Values may be sent and summed in bfloat16 or wider, within the bound.
A program may use at most 128 MiB of HBM per device.

```python
import jax
import jax.numpy as jnp
from jax import lax

D = 12288
HD = 128
GRP = 16
QH = 128
KVH = 8
FF = 26624
ROWS = 64
BATCH = 1024
BLK = 128
POOL = 4
RB = 4
SRC = 8
CAP = 2
N_SECTION = 16


def pool_base(key):
    shape = (KVH, N_SECTION * POOL, BLK, 2 * HD)
    return jnp.clip(jax.random.normal(jax.random.fold_in(key, 101), shape, jnp.float32), -4.0, 4.0)


def pool_table(key):
    return jax.random.randint(jax.random.fold_in(key, 102), (BATCH, RB), 0, POOL).astype(jnp.int32)


def draw_block_table(key, part):
    return pool_table(key)


def draw_kv_pool(key, part):
    base = pool_base(key)
    key_part = base[..., :HD]
    value_part = 4.0 * base[..., HD:]
    return jnp.concatenate([key_part, value_part], axis=-1).astype(jnp.bfloat16)


def draw_queries(key, part):
    shape = (BATCH, QH, HD)
    key = jax.random.fold_in(key, 2)
    values = jnp.clip(jax.random.normal(key, shape, jnp.float32), -4.0, 4.0)
    return values.astype(jnp.bfloat16)


def draw_residual(key, part):
    key = jax.random.fold_in(key, 3)
    row_scale = jnp.exp(jax.random.uniform(jax.random.fold_in(key, 0), (BATCH, 1), jnp.float32, 0.0, 2.3026))
    col_scale = jnp.exp(jax.random.uniform(jax.random.fold_in(key, 1), (1, D), jnp.float32, 0.0, 2.3026))
    trend = (jnp.arange(D).astype(jnp.float32) / D)[None, :]
    rise = jnp.sqrt(1.0 + 2.5 * trend)
    noise = jnp.clip(jax.random.normal(jax.random.fold_in(key, 2), (BATCH, D), jnp.float32), -4.0, 4.0)
    field = 0.05 * row_scale * col_scale * rise * noise
    return field.astype(jnp.bfloat16)


def draw_arrival_section(key, part):
    key = jax.random.fold_in(key, 4)
    busiest = jax.random.randint(jax.random.fold_in(key, 0), (), 0, N_SECTION).astype(jnp.int32)

    def one_source(source):
        source_key = jax.random.fold_in(key, source + 1)
        free_slots = jax.random.permutation(jax.random.fold_in(source_key, 0), (N_SECTION - 1) * CAP)
        others = (free_slots[:SRC - CAP] // CAP).astype(jnp.int32)
        others = others + (others >= busiest).astype(jnp.int32)
        listed = jnp.concatenate([jnp.zeros((CAP,), jnp.int32) + busiest, others])
        shuffle = jax.random.permutation(jax.random.fold_in(source_key, 1), SRC)
        return listed[shuffle]
    return jax.vmap(one_source)(jnp.arange(N_SECTION)).reshape(N_SECTION * SRC).astype(jnp.int32)


def plant(values, own_key, low, largest):
    spot = [jax.random.randint(jax.random.fold_in(own_key, axis), (), 0, length) for axis, length in enumerate(values.shape)]
    widest = values.shape.index(max(values.shape))
    neighbour = spot[:widest] + [(spot[widest] + 1) % values.shape[widest]] + spot[widest + 1:]
    return values.at[tuple(spot)].set(low).at[tuple(neighbour)].set(largest)


def levels(key, shape, cuts, least, top_value):
    gain = 1.0
    for position, shards_of in cuts:
        steps = jax.random.uniform(jax.random.fold_in(jax.random.fold_in(key, 6), position), (shards_of,), jnp.float32, least / len(cuts), top_value / len(cuts))
        gain = gain * jnp.repeat(jnp.exp(steps), shape[position] // shards_of).reshape((-1,) + (1,) * (len(shape) - 1 - position))
    return gain


def bell_draw(stream_key, shape, spread, bound, pieces=(), kind=jnp.bfloat16):
    result = jax.random.normal(stream_key, shape, jnp.float32) * spread
    if len(pieces) > 0:
        result = levels(stream_key, shape, pieces, -0.22, 0.18) * result
    return jnp.clip(result, min=-bound, max=bound).astype(kind)


def setup_inputs(seed: int = 0) -> dict:
    key_list = jax.random.split(jax.random.key(seed), 13)
    queries = draw_queries(jax.random.fold_in(key_list[12], 71), 0)
    kv_pool = draw_kv_pool(jax.random.fold_in(key_list[12], 71), 0)
    block_table = draw_block_table(jax.random.fold_in(key_list[12], 71), 0)
    cached_lengths = plant(jax.random.randint(key_list[3], (BATCH,), 2, RB * BLK + 1), jax.random.fold_in(key_list[3], 1), 2, RB * BLK).astype(jnp.int32)
    arrivals = bell_draw(key_list[4], (KVH, SRC * N_SECTION, BLK, 2 * HD), 1.5, 6.0, ((1, 16),))
    arrival_section = draw_arrival_section(jax.random.fold_in(key_list[12], 71), 0)
    arrival_row = plant(jax.random.randint(key_list[6], (SRC * N_SECTION,), 0, ROWS), jax.random.fold_in(key_list[6], 1), 0, ROWS - 1).astype(jnp.int32)
    out_weight = bell_draw(key_list[7], (QH * HD, D), (QH * HD) ** -0.5, 0.046875, ((0, 16), (1, 16)))
    residual = draw_residual(jax.random.fold_in(key_list[12], 71), 0)
    norm_gain = jnp.clip(1.0 + 0.18 * jax.random.normal(key_list[9], (D,), jnp.float32), 0.099609375, 1.8984375).astype(jnp.bfloat16)
    gate_weight = bell_draw(key_list[10], (D, FF), D ** -0.5, 0.0546875, ((0, 16), (1, 16)))
    up_weight = bell_draw(key_list[11], (D, FF), D ** -0.5, 0.0546875, ((0, 16), (1, 16)))
    return dict(queries=queries, kv_pool=kv_pool, block_table=block_table, cached_lengths=cached_lengths, arrivals=arrivals, arrival_section=arrival_section, arrival_row=arrival_row, out_weight=out_weight, residual=residual, norm_gain=norm_gain, gate_weight=gate_weight, up_weight=up_weight)


NEG_LARGE = -1e+30
EPSILON = 1e-05

def cached_allowed(table_rows, lengths):
    positions = jnp.arange(BLK, dtype=jnp.int32)
    slot_ids = jnp.arange(POOL, dtype=jnp.int32)
    allowed = jnp.zeros((table_rows.shape[0], POOL, BLK), dtype=bool)
    for column in range(RB):
        listed = table_rows[:, column][:, None] == slot_ids[None, :]
        inside = positions[None, :] < (lengths - column * BLK)[:, None]
        allowed = allowed | listed[:, :, None] & inside[:, None, :]
    return allowed.reshape(table_rows.shape[0], POOL * BLK)

def section_attention(section_id, queries, kv_pool, block_table, cached_lengths, arrivals, arrival_section, arrival_row):
    row_first = (section_id * ROWS).astype(jnp.int32)
    row_queries = lax.dynamic_slice_in_dim(queries, row_first, ROWS, 0).astype(jnp.float32).reshape(ROWS, KVH, GRP, HD)
    table_rows = lax.dynamic_slice_in_dim(block_table, row_first, ROWS, 0)
    lengths = lax.dynamic_slice_in_dim(cached_lengths, row_first, ROWS, 0)
    pool_part = lax.dynamic_slice_in_dim(kv_pool, (section_id * POOL).astype(jnp.int32), POOL, 1).reshape(KVH, POOL * BLK, 2 * HD)
    entry_count = N_SECTION * SRC
    entry_ids = jnp.arange(entry_count, dtype=jnp.int32)
    landed = arrival_section == section_id
    ranked = jnp.argsort(jnp.where(landed, entry_ids, entry_ids + entry_count), stable=True).astype(jnp.int32)[:N_SECTION * CAP]
    landed_rows = jnp.where(landed[ranked], arrival_row[ranked], -1)
    gathered = jnp.take(arrivals, ranked, axis=1).reshape(KVH, N_SECTION * CAP * BLK, 2 * HD)
    local_rows = jnp.arange(ROWS, dtype=jnp.int32)
    new_allowed = jnp.repeat(landed_rows[None, :] == local_rows[:, None], BLK, axis=1)
    allowed = jnp.concatenate([cached_allowed(table_rows, lengths), new_allowed], axis=1)
    tokens = jnp.concatenate([pool_part, gathered], axis=1).astype(jnp.float32)
    scores = jnp.einsum('rgqd,gkd->rgqk', row_queries, tokens[:, :, :HD]) * HD ** (-0.5)
    token_mask = allowed[:, None, None, :]
    masked = jnp.where(token_mask, scores, NEG_LARGE)
    highest = lax.optimization_barrier(jnp.max(masked, axis=3, keepdims=True))
    weights = jnp.where(token_mask, jnp.exp(masked - highest), 0.0)
    totals = lax.optimization_barrier(jnp.sum(weights, axis=3))
    rounded = lax.optimization_barrier(weights.astype(jnp.bfloat16)).astype(jnp.float32)
    summed = jnp.einsum('rgqk,gkd->rgqd', rounded, tokens[:, :, HD:])
    return (summed / totals[..., None]).astype(jnp.bfloat16).reshape(ROWS, KVH * GRP * HD)

def reference(queries, kv_pool, block_table, cached_lengths, arrivals, arrival_section, arrival_row, out_weight, residual, norm_gain, gate_weight, up_weight):

    def one_section(section_id):
        return section_attention(section_id, queries, kv_pool, block_table, cached_lengths, arrivals, arrival_section, arrival_row)
    attention = lax.map(one_section, jnp.arange(N_SECTION, dtype=jnp.int32)).reshape(BATCH, QH * HD)
    attn_proj = jnp.dot(attention, out_weight, preferred_element_type=jnp.float32)
    combined = residual.astype(jnp.float32) + attn_proj
    inverse = lax.rsqrt(lax.optimization_barrier(jnp.sum(combined * combined, axis=1, keepdims=True)) / D + EPSILON)
    normed = (combined * norm_gain.astype(jnp.float32)[None, :] * inverse).astype(jnp.bfloat16)
    gate_sums = jnp.dot(normed, gate_weight, preferred_element_type=jnp.float32)
    up_sums = jnp.dot(normed, up_weight, preferred_element_type=jnp.float32)
    hidden = jax.nn.silu(gate_sums) * up_sums
    return (attn_proj, hidden)
```

```python
import functools

import jax
import jax.numpy as jnp
from jax import lax
from jax.experimental import pallas as pl
from jax.experimental.pallas import tpu as pltpu
from jax.sharding import PartitionSpec as P

MESH = pl.DeviceIdType.MESH
CAP = 2
NEG_LARGE = -1e30
EPSILON = 1e-05
VMEM_LIMIT = 60 * 1024 * 1024
BF = jnp.bfloat16
F32 = jnp.float32


def coords():
    s = lax.axis_index("section")
    t = lax.axis_index("tensor")
    return s, t


def section_of(x, y, core):
    return x * 8 + y * 2 + core


def remote(src, dst, ssem, rsem, dev):
    return pltpu.make_async_remote_copy(
        src_ref=src, dst_ref=dst, send_sem=ssem, recv_sem=rsem,
        device_id=dev, device_id_type=MESH)


def signal(sem, dev):
    pl.semaphore_signal(sem, inc=1, device_id=dev, device_id_type=MESH)


def proj_kernel(att, wo, res, gain, proj_out, mg_out, sq_out,
                pz, rbuf, sbuf, xs, xr,
                rs_send, rs_recv, x_send, x_recv, ag_send, ag_recv, agx_send, agx_recv):
    s, t = coords()
    xh, z = t // 8, t % 8
    peer = (s, (1 - xh) * 8 + z)
    right = (s, xh * 8 + (z + 1) % 8)
    left = (s, xh * 8 + (z + 7) % 8)
    ways = (right, left)
    barrier = pltpu.get_barrier_semaphore()
    for dev in (right, left, peer):
        signal(barrier, dev)
    rows = res.shape[0]

    def compute(slot, off):
        zz = (z + off) % 8
        a = jnp.concatenate([att[pl.ds(pl.multiple_of(zz * rows, rows), rows), :],
                             att[pl.ds(pl.multiple_of((8 + zz) * rows, rows), rows), :]], 0)
        p = jnp.dot(a, wo[...], preferred_element_type=F32)
        pz[slot, 0] = p[:rows]
        pz[slot, 1] = p[rows:]

    def off_of(slot):
        k = (slot + 1) // 2
        plus = slot % 2 == 1
        return jnp.where(plus, 4 - k, 4 + k) % 8

    def slot_of(way, k):
        return 0 if k == 0 else 2 * k - 1 + way

    def rs(way, k, h):
        return remote(sbuf.at[way, k, h], rbuf.at[way, k, h],
                      rs_send.at[way, k, h], rs_recv.at[way, k, h], ways[way])

    def send(way, k, h, add):
        v = pz[slot_of(way, k), h]
        if add:
            rs(way, k - 1, h).wait_recv()
            v = v + rbuf[way, k - 1, h].astype(F32)
        sbuf[way, k, h] = v.astype(BF)
        rs(way, k, h).start()

    compute(0, 4)
    pl.semaphore_wait(barrier, 3)
    for way in (0, 1):
        send(way, 0, way, False)

    def group(lo, hi):
        @pl.loop(lo, hi)
        def _(i):
            compute(i, off_of(i))

    group(1, 3)
    for way in (0, 1):
        send(way, 1, 1 - way, False)
    group(3, 8)
    for k in (1, 2, 3):
        for way in (0, 1):
            if k == 1:
                send(way, 1, way, True)
            else:
                send(way, k, 1 - way, True)
        if k > 1:
            for way in (0, 1):
                send(way, k, way, True)

    def total(h):
        for way in (0, 1):
            rs(way, 3, h).wait_recv()
        return pz[7, h] + rbuf[0, 3, h].astype(F32) + rbuf[1, 3, h].astype(F32)

    def xcopy():
        return remote(xs, xr, x_send, x_recv, peer)

    xs[...] = total(1 - xh).astype(BF)
    xcopy().start()
    proj_out[...] = total(xh)
    xcopy().wait_recv()
    proj = proj_out[...] + xr[...].astype(F32)
    proj_out[...] = proj
    mixed = proj + res[...].astype(F32)
    own = xh * 8 + z
    mg_out[own] = (mixed * gain[...].astype(F32)).astype(BF)

    def agx():
        return remote(mg_out.at[own], mg_out.at[own], agx_send, agx_recv, peer)

    def ag(way, k, h):
        hh = xh if h == 0 else 1 - xh
        zz = (z - k + 8) % 8 if way == 0 else (z + k) % 8
        blk = hh * 8 + zz
        return remote(mg_out.at[blk], mg_out.at[blk], ag_send.at[way, k, h], ag_recv.at[way, k, h], ways[way])

    for way in (0, 1):
        ag(way, 0, 0).start()
    agx().start()
    sq_out[...] = jnp.sum(mixed * mixed, axis=1, keepdims=True) + jnp.zeros(sq_out.shape, F32)
    agx().wait_recv()
    for way in (0, 1):
        ag(way, 0, 1).start()
    for k in (1, 2):
        for h in (0, 1):
            for way in (0, 1):
                ag(way, k - 1, h).wait_recv()
                ag(way, k, h).start()
    def ag_last(way):
        blk = way * 8 + ((z + 5) % 8 if way == 0 else (z + 3) % 8)
        return remote(mg_out.at[blk], mg_out.at[blk], ag_send.at[way, 3, 0], ag_recv.at[way, 3, 0], ways[way])

    for way in (0, 1):
        for h in (0, 1):
            ag(way, 2, h).wait_recv()
        ag_last(way).start()
    for way in (0, 1):
        ag_last(way).wait_recv()
        ag_last(way).wait_send()
    for way in (0, 1):
        for k in range(4):
            for h in (0, 1):
                if k == 0 and h != way:
                    continue
                rs(way, k, h).wait_send()
        for k in range(3):
            for h in (0, 1):
                ag(way, k, h).wait_send()
    xcopy().wait_send()
    agx().wait_send()


def proj_call(att, wo, res, gain):
    rows, width = res.shape
    dma = pltpu.SemaphoreType.DMA
    vm = pl.BlockSpec(memory_space=pltpu.VMEM)
    return pl.pallas_call(
        proj_kernel,
        out_shape=(jax.ShapeDtypeStruct((rows, width), F32),
                   jax.ShapeDtypeStruct((16, rows, width), BF),
                   jax.ShapeDtypeStruct((rows, 128), F32)),
        in_specs=[vm] * 4,
        out_specs=(vm,) * 3,
        scratch_shapes=[
            pltpu.VMEM((8, 2, rows, width), F32),
            pltpu.VMEM((2, 4, 2, rows, width), BF),
            pltpu.VMEM((2, 4, 2, rows, width), BF),
            pltpu.VMEM((rows, width), BF),
            pltpu.VMEM((rows, width), BF),
            dma((2, 4, 2)), dma((2, 4, 2)), dma, dma,
            dma((2, 4, 2)), dma((2, 4, 2)), dma, dma,
        ],
        compiler_params=pltpu.CompilerParams(
            collective_id=1, has_side_effects=True, vmem_limit_bytes=VMEM_LIMIT),
        name="projection",
    )(att, wo, res, gain)


def ffn_kernel(mg, gate, up, sq, hid,
               wf, mgf, pb, pa, bs, br, as_, ar, xas, xar, xbs, xbr, ps, pr, sqr, fin,
               w_sem, m_sem, ws, wr, ms, mr,
               bss, brs, ass, ars, xass, xars, xbss, xbrs, pss, prs, sqs, sqrs, dgs, dgr):
    s, t = coords()
    x, y, core = s // 8, (s // 2) % 4, s % 2
    mate = (section_of(x, y, 1 - core), t)
    xpeer = (section_of(1 - x, y, core), t)
    yp = (section_of(x, (y + 1) % 4, core), t)
    ym = (section_of(x, (y + 3) % 4, core), t)
    ways = (yp, ym)
    diag = s == t
    n = 16
    FFN = gate.shape[1]
    CA = xar.shape[2]
    CB = FFN - CA
    H = CA // 2
    R = 128
    width = gate.shape[0]
    barrier = pltpu.get_barrier_semaphore()
    for dev in (mate, xpeer, yp, ym):
        signal(barrier, dev)

    @pl.when(diag)
    def _():
        for i in range(1, n):
            signal(barrier, ((s + i) % n, t))

    @pl.when(jnp.logical_not(diag))
    def _():
        signal(barrier, (s, s))

    def w_own(c):
        return pltpu.make_async_copy(gate if c == 0 else up, wf.at[c], w_sem)

    def m_own():
        return pltpu.make_async_copy(mg, mgf.at[core], m_sem)

    for c in (0, 1):
        @pl.when(core == c)
        def _():
            w_own(c).start()
    m_own().start()

    @pl.when(diag)
    def _():
        pl.semaphore_wait(barrier, 4 + n - 1)

    @pl.when(jnp.logical_not(diag))
    def _():
        pl.semaphore_wait(barrier, 5)

    def w_far(c):
        return remote(up if c == 0 else gate, wf.at[c], ws, wr, mate)

    def m_far():
        return remote(mg, mgf.at[core], ms, mr, mate)

    m_far().start()
    for c in (0, 1):
        @pl.when(core == c)
        def _():
            w_far(c).start()

    def sq_copy(slot):
        return remote(sq, sqr.at[slot], sqs, sqrs.at[slot], (t, t))

    def dg_copy(i):
        return remote(fin, fin, dgs.at[i], dgr, (s, (t + i) % n))

    @pl.when(jnp.logical_not(diag))
    def _():
        sq_copy((s - t + n) % n).start()

    for c in (0, 1):
        @pl.when(core == c)
        def _():
            w_own(c).wait()
    m_own().wait()
    m_far().wait_recv()
    for c in (0, 1):
        @pl.when(core == c)
        def _():
            w_far(c).wait_recv()

    def part(xx, yy, c0, cn):
        r0 = pl.multiple_of((xx * 4 + yy) * R, R)
        return (jnp.dot(mgf[0, pl.ds(r0, R), :], wf[0, :, c0:c0 + cn], preferred_element_type=F32)
                + jnp.dot(mgf[1, pl.ds(r0, R), :], wf[1, :, c0:c0 + cn], preferred_element_type=F32))

    def yoff(k):
        return (y + jnp.where(k == 0, 2, jnp.where(k == 1, 1, jnp.where(k == 2, 3, 0)))) % 4

    def b_group(lo, hi):
        @pl.loop(lo, hi)
        def _(i):
            pb[i] = part(i % 2, yoff(i // 2), CA, CB)

    def a_group(xx, base, lo, hi):
        @pl.loop(lo, hi)
        def _(i):
            pa[base + i] = part(xx, yoff(i), 0, CA)

    def bcopy(way, m):
        return remote(bs.at[way, m], br.at[way, m], bss.at[way, m], brs.at[way, m], ways[way])

    def acopy(way, m):
        return remote(as_.at[way, m], ar.at[way, m], ass.at[way, m], ars.at[way, m], ways[way])

    def xacopy(k):
        return remote(xas.at[k], xar.at[k], xass.at[k], xars.at[k], xpeer)

    def xbcopy():
        return remote(xbs, xbr, xbss, xbrs, xpeer)

    def xa_send(k):
        xas[k] = pa[4 + k].astype(BF)
        xacopy(k).start()

    b_group(0, 2)
    for way in (0, 1):
        bs[way, 0] = pb[way].astype(BF)
        bcopy(way, 0).start()
    a_group(1 - x, 4, 0, 1)
    xa_send(0)
    b_group(2, 6)
    for way in (0, 1):
        bs[way, 1] = pb[2 * (1 + way) + 1 - way].astype(BF)
        bcopy(way, 1).start()
    a_group(1 - x, 4, 1, 4)
    for k in (1, 2, 3):
        xa_send(k)
    for way in (0, 1):
        bcopy(way, 0).wait_recv()
        bs[way, 2] = (pb[2 * (1 + way) + way] + br[way, 0].astype(F32)).astype(BF)
        bcopy(way, 2).start()
    a_group(x, 0, 0, 4)
    b_group(6, 8)

    def a_sum(k):
        xacopy(k).wait_recv()
        pa[k] = pa[k] + xar[k].astype(F32)

    a_sum(0)
    for way in (0, 1):
        as_[way, 0] = pa[0, :, way * H:(way + 1) * H].astype(BF)
        acopy(way, 0).start()
    for k in (1, 2):
        a_sum(k)
        way = k - 1
        as_[way, 1] = pa[k, :, (1 - way) * H:(2 - way) * H].astype(BF)
        acopy(way, 1).start()
    for way in (0, 1):
        acopy(way, 0).wait_recv()
        as_[way, 2] = (pa[1 + way, :, way * H:(way + 1) * H] + ar[way, 0].astype(F32)).astype(BF)
        acopy(way, 2).start()

    for way in (0, 1):
        bcopy(way, 1).wait_recv()
        bcopy(way, 2).wait_recv()
    for h in (0, 1):
        pb[6 + h] = pb[6 + h] + br[h, 2].astype(F32) + br[1 - h, 1].astype(F32)
    xbs[...] = pb[6 + 1 - x].astype(BF)
    xbcopy().start()

    @pl.when(diag)
    def _():
        acc = sq[...]
        for i in range(1, n):
            sq_copy(i).wait_recv()
            acc = acc + sqr[i]
        fin[...] = acc
        for i in range(1, n):
            dg_copy(i).start()

    a_sum(3)
    for way in (0, 1):
        acopy(way, 1).wait_recv()
        acopy(way, 2).wait_recv()
    for h in (0, 1):
        pa[3, :, h * H:(h + 1) * H] = (pa[3, :, h * H:(h + 1) * H]
                                       + ar[h, 2].astype(F32) + ar[1 - h, 1].astype(F32))

    HR = R // 2
    give = pl.multiple_of((1 - core) * HR, HR)
    keep = pl.multiple_of(core * HR, HR)

    def pcopy(i):
        return remote(ps.at[i], pr.at[i], pss.at[i], prs.at[i], mate)

    ps[0, :, :CA] = pa[3, pl.ds(give, HR), :]
    pcopy(0).start()
    xbcopy().wait_recv()
    own = pb[6 + x] + xbr[...].astype(F32)
    pb[6] = own
    ps[1, :, :CB] = pb[6, pl.ds(give, HR), :]
    pcopy(1).start()

    @pl.when(jnp.logical_not(diag))
    def _():
        dg_copy(1).wait_recv()

    inv = lax.rsqrt(fin[:, :1] / (width * n) + EPSILON)

    def finish(i, mine, c0, cn):
        pcopy(i).wait_recv()
        other = pr[i, :, :cn] * inv
        mine = mine * inv
        g = jnp.where(core == 0, mine, other)
        u = jnp.where(core == 0, other, mine)
        hid[:, c0:c0 + cn] = g / (1.0 + jnp.exp(-g)) * u

    finish(0, pa[3, pl.ds(keep, HR), :], 0, CA)
    finish(1, pb[6, pl.ds(keep, HR), :], CA, CB)

    for way in (0, 1):
        for m in (0, 1, 2):
            bcopy(way, m).wait_send()
            acopy(way, m).wait_send()
    for k in range(4):
        xacopy(k).wait_send()
    xbcopy().wait_send()
    for i in (0, 1):
        pcopy(i).wait_send()
    m_far().wait_send()
    for c in (0, 1):
        @pl.when(core == c)
        def _():
            w_far(c).wait_send()

    @pl.when(diag)
    def _():
        for i in range(1, n):
            dg_copy(i).wait_send()

    @pl.when(jnp.logical_not(diag))
    def _():
        sq_copy((s - t + n) % n).wait_send()


def ffn_call(mg, gate, up, sq):
    width, ffn = gate.shape
    rows = sq.shape[0]
    ca = 6 * 128
    cb = ffn - ca
    dma = pltpu.SemaphoreType.DMA
    vm = pl.BlockSpec(memory_space=pltpu.VMEM)
    hbm = pl.BlockSpec(memory_space=pl.ANY)
    return pl.pallas_call(
        ffn_kernel,
        out_shape=jax.ShapeDtypeStruct((rows, ffn), F32),
        in_specs=[hbm, hbm, hbm, vm],
        out_specs=vm,
        scratch_shapes=[
            pltpu.VMEM((2, width, ffn), BF),
            pltpu.VMEM((2, 16 * rows, width), BF),
            pltpu.VMEM((8, 128, cb), F32),
            pltpu.VMEM((8, 128, ca), F32),
            pltpu.VMEM((2, 3, 128, cb), BF),
            pltpu.VMEM((2, 3, 128, cb), BF),
            pltpu.VMEM((2, 3, 128, ca // 2), BF),
            pltpu.VMEM((2, 3, 128, ca // 2), BF),
            pltpu.VMEM((4, 128, ca), BF),
            pltpu.VMEM((4, 128, ca), BF),
            pltpu.VMEM((128, cb), BF),
            pltpu.VMEM((128, cb), BF),
            pltpu.VMEM((2, 64, cb), F32),
            pltpu.VMEM((2, 64, cb), F32),
            pltpu.VMEM((16, rows, 128), F32),
            pltpu.VMEM((rows, 128), F32),
            dma, dma, dma, dma, dma, dma,
            dma((2, 3)), dma((2, 3)), dma((2, 3)), dma((2, 3)),
            dma((4,)), dma((4,)), dma, dma, dma((2,)), dma((2,)),
            dma, dma((16,)), dma((16,)), dma,
        ],
        compiler_params=pltpu.CompilerParams(
            collective_id=2, has_side_effects=True, vmem_limit_bytes=VMEM_LIMIT),
        name="ffn",
    )(mg, gate, up, sq)


def cached_allowed(table_rows, lengths, slot_count, block_len):
    positions = jnp.arange(block_len)
    slot_ids = jnp.arange(slot_count)
    allowed = jnp.zeros((table_rows.shape[0], slot_count, block_len), dtype=bool)
    for column in range(table_rows.shape[1]):
        listed = table_rows[:, column][:, None] == slot_ids[None, :]
        inside = positions[None, :] < (lengths - column * block_len)[:, None]
        allowed = allowed | listed[:, :, None] & inside[:, None, :]
    return allowed.reshape(table_rows.shape[0], slot_count * block_len)


def partial_softmax(queries, tokens, allowed):
    head_dim = queries.shape[2]
    scores = jnp.einsum(
        "rhd,kd->rhk", queries, tokens[:, :head_dim], preferred_element_type=jnp.float32
    ) * head_dim ** (-0.5)
    token_mask = allowed[:, None, :]
    masked = jnp.where(token_mask, scores, NEG_LARGE)
    highest = jnp.max(masked, axis=2)
    weights = jnp.where(token_mask, jnp.exp(masked - highest[:, :, None]), 0.0)
    totals = jnp.sum(weights, axis=2)
    summed = jnp.einsum(
        "rhk,kd->rhd",
        weights.astype(jnp.bfloat16),
        tokens[:, head_dim:],
        preferred_element_type=jnp.float32,
    )
    return (highest, totals, summed)


def body(
    queries,
    kv_pool,
    block_table,
    cached_lengths,
    arrivals,
    arrival_section,
    arrival_row,
    out_weight,
    residual,
    norm_gain,
    gate_weight,
    up_weight,
):
    sections = lax.axis_size("section")
    tensor_id = lax.axis_index("tensor")
    kv_group = tensor_id // 2
    row_count = queries.shape[0]
    slot_count = kv_pool.shape[1]
    block_len = kv_pool.shape[2]
    features = kv_pool.shape[3]
    own_pool = lax.dynamic_index_in_dim(kv_pool, kv_group, 0, keepdims=False).reshape(
        slot_count * block_len, features
    )
    pool_allowed = cached_allowed(block_table, cached_lengths, slot_count, block_len)
    own_new = lax.dynamic_index_in_dim(arrivals, kv_group, 0, keepdims=False)
    sources = own_new.shape[0]
    entry_ids = jnp.arange(sources)
    same_dest = arrival_section[:, None] == arrival_section[None, :]
    earlier = same_dest & (entry_ids[None, :] < entry_ids[:, None])
    slot_rank = jnp.sum(earlier.astype(jnp.int32), axis=1)
    target = arrival_section * CAP + slot_rank
    placing = jnp.arange(sections * CAP)[:, None] == target[None, :]
    send_blocks = jnp.dot(
        placing.astype(jnp.bfloat16),
        own_new.reshape(sources, block_len * features),
        preferred_element_type=jnp.bfloat16,
    )
    send_blocks = send_blocks.reshape(sections, CAP, block_len, features)
    send_rows = (jnp.sum(jnp.where(placing, arrival_row[None, :] + 1, 0), axis=1) - 1).reshape(
        sections, CAP
    )
    got_blocks, got_rows = (
        lax.all_to_all(send_blocks, "section", split_axis=0, concat_axis=0, tiled=True),
        lax.all_to_all(send_rows, "section", split_axis=0, concat_axis=0, tiled=True),
    )
    arrived = got_blocks.reshape(sections * CAP * block_len, features)
    owner_match = got_rows.reshape(sections * CAP)[None, :] == jnp.arange(row_count)[:, None]
    new_allowed = jnp.broadcast_to(
        owner_match[:, :, None], (row_count, sections * CAP, block_len)
    ).reshape(row_count, sections * CAP * block_len)
    highest, totals, summed = partial_softmax(
        queries,
        jnp.concatenate([own_pool, arrived], 0),
        jnp.concatenate([pool_allowed, new_allowed], 1),
    )
    attention = (summed / totals[:, :, None]).astype(jnp.bfloat16).reshape(row_count, -1)
    att = lax.all_gather(attention, "section", axis=0, tiled=True)
    attn_proj, mg, sq = proj_call(att, out_weight, residual, norm_gain.reshape(1, -1))
    hidden = ffn_call(mg.reshape(-1, mg.shape[2]), gate_weight, up_weight, sq)
    return (attn_proj, hidden)


def solution(mesh):
    placed = (
        P("section", "tensor", None),
        P(None, "section", None, None),
        P("section", None),
        P("section"),
        P(None, "section", None, None),
        P("section"),
        P("section"),
        P("tensor", "section"),
        P("tensor", "section"),
        P("section"),
        P("section", "tensor"),
        P("section", "tensor"),
    )
    return jax.shard_map(
        body,
        mesh=mesh,
        in_specs=placed,
        out_specs=(P("tensor", "section"), P("section", "tensor")),
        check_vma=False,
    )
```

```python
import functools

import jax
import jax.numpy as jnp
from jax import lax
from jax.experimental import pallas as pl
from jax.experimental.pallas import tpu as pltpu
from jax.sharding import PartitionSpec as P

MESH = pl.DeviceIdType.MESH
CAP = 2
NEG_LARGE = -1e30
EPSILON = 1e-05
VMEM_LIMIT = 60 * 1024 * 1024
BF = jnp.bfloat16
F32 = jnp.float32


def coords():
    s = lax.axis_index("section")
    t = lax.axis_index("tensor")
    return s, t


def section_of(x, y, core):
    return x * 8 + y * 2 + core


def remote(src, dst, ssem, rsem, dev):
    return pltpu.make_async_remote_copy(
        src_ref=src, dst_ref=dst, send_sem=ssem, recv_sem=rsem,
        device_id=dev, device_id_type=MESH)


def signal(sem, dev):
    pl.semaphore_signal(sem, inc=1, device_id=dev, device_id_type=MESH)


def proj_kernel(att, wo, res, gain, proj_out, mg_out, sq_out,
                pz, rbuf, sbuf, xs, xr,
                rs_send, rs_recv, x_send, x_recv, ag_send, ag_recv, agx_send, agx_recv):
    s, t = coords()
    xh, z = t // 8, t % 8
    peer = (s, (1 - xh) * 8 + z)
    right = (s, xh * 8 + (z + 1) % 8)
    left = (s, xh * 8 + (z + 7) % 8)
    ways = (right, left)
    barrier = pltpu.get_barrier_semaphore()
    for dev in (right, left, peer):
        signal(barrier, dev)
    rows = res.shape[0]

    def compute(slot, off):
        zz = (z + off) % 8
        a = jnp.concatenate([att[pl.ds(pl.multiple_of(zz * rows, rows), rows), :],
                             att[pl.ds(pl.multiple_of((8 + zz) * rows, rows), rows), :]], 0)
        p = jnp.dot(a, wo[...], preferred_element_type=F32)
        pz[slot, 0] = p[:rows]
        pz[slot, 1] = p[rows:]

    def off_of(slot):
        k = (slot + 1) // 2
        plus = slot % 2 == 1
        return jnp.where(plus, 4 - k, 4 + k) % 8

    def slot_of(way, k):
        return 0 if k == 0 else 2 * k - 1 + way

    def rs(way, k, h):
        return remote(sbuf.at[way, k, h], rbuf.at[way, k, h],
                      rs_send.at[way, k, h], rs_recv.at[way, k, h], ways[way])

    def send(way, k, h, add):
        v = pz[slot_of(way, k), h]
        if add:
            rs(way, k - 1, h).wait_recv()
            v = v + rbuf[way, k - 1, h].astype(F32)
        sbuf[way, k, h] = v.astype(BF)
        rs(way, k, h).start()

    compute(0, 4)
    pl.semaphore_wait(barrier, 3)
    for way in (0, 1):
        send(way, 0, way, False)

    def group(lo, hi):
        @pl.loop(lo, hi)
        def _(i):
            compute(i, off_of(i))

    group(1, 3)
    for way in (0, 1):
        send(way, 1, 1 - way, False)
    group(3, 8)
    for k in (1, 2, 3):
        for way in (0, 1):
            if k == 1:
                send(way, 1, way, True)
            else:
                send(way, k, 1 - way, True)
        if k > 1:
            for way in (0, 1):
                send(way, k, way, True)

    def total(h):
        for way in (0, 1):
            rs(way, 3, h).wait_recv()
        return pz[7, h] + rbuf[0, 3, h].astype(F32) + rbuf[1, 3, h].astype(F32)

    def xcopy():
        return remote(xs, xr, x_send, x_recv, peer)

    xs[...] = total(1 - xh).astype(BF)
    xcopy().start()
    proj_out[...] = total(xh)
    xcopy().wait_recv()
    proj = proj_out[...] + xr[...].astype(F32)
    proj_out[...] = proj
    mixed = proj + res[...].astype(F32)
    own = xh * 8 + z
    mg_out[own] = (mixed * gain[...].astype(F32)).astype(BF)

    def agx():
        return remote(mg_out.at[own], mg_out.at[own], agx_send, agx_recv, peer)

    def ag(way, k, h):
        hh = xh if h == 0 else 1 - xh
        zz = (z - k + 8) % 8 if way == 0 else (z + k) % 8
        blk = hh * 8 + zz
        return remote(mg_out.at[blk], mg_out.at[blk], ag_send.at[way, k, h], ag_recv.at[way, k, h], ways[way])

    for way in (0, 1):
        ag(way, 0, 0).start()
    agx().start()
    sq_out[...] = jnp.sum(mixed * mixed, axis=1, keepdims=True) + jnp.zeros(sq_out.shape, F32)
    agx().wait_recv()
    for way in (0, 1):
        ag(way, 0, 1).start()
    for k in (1, 2):
        for h in (0, 1):
            for way in (0, 1):
                ag(way, k - 1, h).wait_recv()
                ag(way, k, h).start()
    def ag_last(way):
        blk = way * 8 + ((z + 5) % 8 if way == 0 else (z + 3) % 8)
        return remote(mg_out.at[blk], mg_out.at[blk], ag_send.at[way, 3, 0], ag_recv.at[way, 3, 0], ways[way])

    for way in (0, 1):
        for h in (0, 1):
            ag(way, 2, h).wait_recv()
        ag_last(way).start()
    for way in (0, 1):
        ag_last(way).wait_recv()
        ag_last(way).wait_send()
    for way in (0, 1):
        for k in range(4):
            for h in (0, 1):
                if k == 0 and h != way:
                    continue
                rs(way, k, h).wait_send()
        for k in range(3):
            for h in (0, 1):
                ag(way, k, h).wait_send()
    xcopy().wait_send()
    agx().wait_send()


def proj_call(att, wo, res, gain):
    rows, width = res.shape
    dma = pltpu.SemaphoreType.DMA
    vm = pl.BlockSpec(memory_space=pltpu.VMEM)
    return pl.pallas_call(
        proj_kernel,
        out_shape=(jax.ShapeDtypeStruct((rows, width), F32),
                   jax.ShapeDtypeStruct((16, rows, width), BF),
                   jax.ShapeDtypeStruct((rows, 128), F32)),
        in_specs=[vm] * 4,
        out_specs=(vm,) * 3,
        scratch_shapes=[
            pltpu.VMEM((8, 2, rows, width), F32),
            pltpu.VMEM((2, 4, 2, rows, width), BF),
            pltpu.VMEM((2, 4, 2, rows, width), BF),
            pltpu.VMEM((rows, width), BF),
            pltpu.VMEM((rows, width), BF),
            dma((2, 4, 2)), dma((2, 4, 2)), dma, dma,
            dma((2, 4, 2)), dma((2, 4, 2)), dma, dma,
        ],
        compiler_params=pltpu.CompilerParams(
            collective_id=1, has_side_effects=True, vmem_limit_bytes=VMEM_LIMIT),
        name="projection",
    )(att, wo, res, gain)


def ffn_kernel(mg, gate, up, sq, hid,
               wf, mgf, pb, pa, bs, br, as_, ar, xas, xar, xbs, xbr, ps, pr, sqr, fin,
               w_sem, m_sem, ws, wr, ms, mr,
               bss, brs, ass, ars, xass, xars, xbss, xbrs, pss, prs, sqs, sqrs, dgs, dgr):
    s, t = coords()
    x, y, core = s // 8, (s // 2) % 4, s % 2
    mate = (section_of(x, y, 1 - core), t)
    xpeer = (section_of(1 - x, y, core), t)
    yp = (section_of(x, (y + 1) % 4, core), t)
    ym = (section_of(x, (y + 3) % 4, core), t)
    ways = (yp, ym)
    diag = s == t
    n = 16
    FFN = gate.shape[1]
    CA = xar.shape[2]
    CB = FFN - CA
    H = CA // 2
    R = 128
    width = gate.shape[0]
    barrier = pltpu.get_barrier_semaphore()
    for dev in (mate, xpeer, yp, ym):
        signal(barrier, dev)

    @pl.when(diag)
    def _():
        for i in range(1, n):
            signal(barrier, ((s + i) % n, t))

    @pl.when(jnp.logical_not(diag))
    def _():
        signal(barrier, (s, s))

    def w_own(c):
        return pltpu.make_async_copy(gate if c == 0 else up, wf.at[c], w_sem)

    def m_own():
        return pltpu.make_async_copy(mg, mgf.at[core], m_sem)

    for c in (0, 1):
        @pl.when(core == c)
        def _():
            w_own(c).start()
    m_own().start()

    @pl.when(diag)
    def _():
        pl.semaphore_wait(barrier, 4 + n - 1)

    @pl.when(jnp.logical_not(diag))
    def _():
        pl.semaphore_wait(barrier, 5)

    def w_far(c):
        return remote(up if c == 0 else gate, wf.at[c], ws, wr, mate)

    def m_far():
        return remote(mg, mgf.at[core], ms, mr, mate)

    m_far().start()
    for c in (0, 1):
        @pl.when(core == c)
        def _():
            w_far(c).start()

    def sq_copy(slot):
        return remote(sq, sqr.at[slot], sqs, sqrs.at[slot], (t, t))

    def dg_copy(i):
        return remote(fin, fin, dgs.at[i], dgr, (s, (t + i) % n))

    @pl.when(jnp.logical_not(diag))
    def _():
        sq_copy((s - t + n) % n).start()

    for c in (0, 1):
        @pl.when(core == c)
        def _():
            w_own(c).wait()
    m_own().wait()
    m_far().wait_recv()
    for c in (0, 1):
        @pl.when(core == c)
        def _():
            w_far(c).wait_recv()

    def part(xx, yy, c0, cn):
        r0 = pl.multiple_of((xx * 4 + yy) * R, R)
        return (jnp.dot(mgf[0, pl.ds(r0, R), :], wf[0, :, c0:c0 + cn], preferred_element_type=F32)
                + jnp.dot(mgf[1, pl.ds(r0, R), :], wf[1, :, c0:c0 + cn], preferred_element_type=F32))

    def yoff(k):
        return (y + jnp.where(k == 0, 2, jnp.where(k == 1, 1, jnp.where(k == 2, 3, 0)))) % 4

    def b_group(lo, hi):
        @pl.loop(lo, hi)
        def _(i):
            pb[i] = part(i % 2, yoff(i // 2), CA, CB)

    def a_group(xx, base, lo, hi):
        @pl.loop(lo, hi)
        def _(i):
            pa[base + i] = part(xx, yoff(i), 0, CA)

    def bcopy(way, m):
        return remote(bs.at[way, m], br.at[way, m], bss.at[way, m], brs.at[way, m], ways[way])

    def acopy(way, m):
        return remote(as_.at[way, m], ar.at[way, m], ass.at[way, m], ars.at[way, m], ways[way])

    def xacopy(k):
        return remote(xas.at[k], xar.at[k], xass.at[k], xars.at[k], xpeer)

    def xbcopy():
        return remote(xbs, xbr, xbss, xbrs, xpeer)

    def xa_send(k):
        xas[k] = pa[4 + k].astype(BF)
        xacopy(k).start()

    b_group(0, 2)
    for way in (0, 1):
        bs[way, 0] = pb[way].astype(BF)
        bcopy(way, 0).start()
    a_group(1 - x, 4, 0, 1)
    xa_send(0)
    b_group(2, 6)
    for way in (0, 1):
        bs[way, 1] = pb[2 * (1 + way) + 1 - way].astype(BF)
        bcopy(way, 1).start()
    a_group(1 - x, 4, 1, 4)
    for k in (1, 2, 3):
        xa_send(k)
    for way in (0, 1):
        bcopy(way, 0).wait_recv()
        bs[way, 2] = (pb[2 * (1 + way) + way] + br[way, 0].astype(F32)).astype(BF)
        bcopy(way, 2).start()
    a_group(x, 0, 0, 4)
    b_group(6, 8)

    def a_sum(k):
        xacopy(k).wait_recv()
        pa[k] = pa[k] + xar[k].astype(F32)

    a_sum(0)
    for way in (0, 1):
        as_[way, 0] = pa[0, :, way * H:(way + 1) * H].astype(BF)
        acopy(way, 0).start()
    for k in (1, 2):
        a_sum(k)
        way = k - 1
        as_[way, 1] = pa[k, :, (1 - way) * H:(2 - way) * H].astype(BF)
        acopy(way, 1).start()
    for way in (0, 1):
        acopy(way, 0).wait_recv()
        as_[way, 2] = (pa[1 + way, :, way * H:(way + 1) * H] + ar[way, 0].astype(F32)).astype(BF)
        acopy(way, 2).start()

    for way in (0, 1):
        bcopy(way, 1).wait_recv()
        bcopy(way, 2).wait_recv()
    for h in (0, 1):
        pb[6 + h] = pb[6 + h] + br[h, 2].astype(F32) + br[1 - h, 1].astype(F32)
    xbs[...] = pb[6 + 1 - x].astype(BF)
    xbcopy().start()

    @pl.when(diag)
    def _():
        acc = sq[...]
        for i in range(1, n):
            sq_copy(i).wait_recv()
            acc = acc + sqr[i]
        fin[...] = acc
        for i in range(1, n):
            dg_copy(i).start()

    a_sum(3)
    for way in (0, 1):
        acopy(way, 1).wait_recv()
        acopy(way, 2).wait_recv()
    for h in (0, 1):
        pa[3, :, h * H:(h + 1) * H] = (pa[3, :, h * H:(h + 1) * H]
                                       + ar[h, 2].astype(F32) + ar[1 - h, 1].astype(F32))

    HR = R // 2
    give = pl.multiple_of((1 - core) * HR, HR)
    keep = pl.multiple_of(core * HR, HR)

    def pcopy(i):
        return remote(ps.at[i], pr.at[i], pss.at[i], prs.at[i], mate)

    ps[0, :, :CA] = pa[3, pl.ds(give, HR), :]
    pcopy(0).start()
    xbcopy().wait_recv()
    own = pb[6 + x] + xbr[...].astype(F32)
    pb[6] = own
    ps[1, :, :CB] = pb[6, pl.ds(give, HR), :]
    pcopy(1).start()

    @pl.when(jnp.logical_not(diag))
    def _():
        dg_copy(1).wait_recv()

    inv = lax.rsqrt(fin[:, :1] / (width * n) + EPSILON)

    def finish(i, mine, c0, cn):
        pcopy(i).wait_recv()
        other = pr[i, :, :cn] * inv
        mine = mine * inv
        g = jnp.where(core == 0, mine, other)
        u = jnp.where(core == 0, other, mine)
        hid[:, c0:c0 + cn] = g / (1.0 + jnp.exp(-g)) * u

    finish(0, pa[3, pl.ds(keep, HR), :], 0, CA)
    finish(1, pb[6, pl.ds(keep, HR), :], CA, CB)

    for way in (0, 1):
        for m in (0, 1, 2):
            bcopy(way, m).wait_send()
            acopy(way, m).wait_send()
    for k in range(4):
        xacopy(k).wait_send()
    xbcopy().wait_send()
    for i in (0, 1):
        pcopy(i).wait_send()
    m_far().wait_send()
    for c in (0, 1):
        @pl.when(core == c)
        def _():
            w_far(c).wait_send()

    @pl.when(diag)
    def _():
        for i in range(1, n):
            dg_copy(i).wait_send()

    @pl.when(jnp.logical_not(diag))
    def _():
        sq_copy((s - t + n) % n).wait_send()


def ffn_call(mg, gate, up, sq):
    width, ffn = gate.shape
    rows = sq.shape[0]
    ca = 6 * 128
    cb = ffn - ca
    dma = pltpu.SemaphoreType.DMA
    vm = pl.BlockSpec(memory_space=pltpu.VMEM)
    hbm = pl.BlockSpec(memory_space=pl.ANY)
    return pl.pallas_call(
        ffn_kernel,
        out_shape=jax.ShapeDtypeStruct((rows, ffn), F32),
        in_specs=[hbm, hbm, hbm, vm],
        out_specs=vm,
        scratch_shapes=[
            pltpu.VMEM((2, width, ffn), BF),
            pltpu.VMEM((2, 16 * rows, width), BF),
            pltpu.VMEM((8, 128, cb), F32),
            pltpu.VMEM((8, 128, ca), F32),
            pltpu.VMEM((2, 3, 128, cb), BF),
            pltpu.VMEM((2, 3, 128, cb), BF),
            pltpu.VMEM((2, 3, 128, ca // 2), BF),
            pltpu.VMEM((2, 3, 128, ca // 2), BF),
            pltpu.VMEM((4, 128, ca), BF),
            pltpu.VMEM((4, 128, ca), BF),
            pltpu.VMEM((128, cb), BF),
            pltpu.VMEM((128, cb), BF),
            pltpu.VMEM((2, 64, cb), F32),
            pltpu.VMEM((2, 64, cb), F32),
            pltpu.VMEM((16, rows, 128), F32),
            pltpu.VMEM((rows, 128), F32),
            dma, dma, dma, dma, dma, dma,
            dma((2, 3)), dma((2, 3)), dma((2, 3)), dma((2, 3)),
            dma((4,)), dma((4,)), dma, dma, dma((2,)), dma((2,)),
            dma, dma((16,)), dma((16,)), dma,
        ],
        compiler_params=pltpu.CompilerParams(
            collective_id=2, has_side_effects=True, vmem_limit_bytes=VMEM_LIMIT),
        name="ffn",
    )(mg, gate, up, sq)


def softmax_parts(q, k, v, allowed):
    s = lax.dot_general(q, k, (((1,), (1,)), ((), ())), preferred_element_type=F32) * (q.shape[1] ** -0.5)
    s = jnp.where(allowed, s, NEG_LARGE)
    m = jnp.max(s, axis=1, keepdims=True)
    p = jnp.where(allowed, jnp.exp(s - m), 0.0)
    l = jnp.sum(p, axis=1, keepdims=True)
    o = jnp.dot(p.astype(BF), v, preferred_element_type=F32)
    return m, l, o


def attn_kernel(sec, row, q, tab, pool, arr, att,
                kvp, kva, tb, tr, qs, qr, rb, rr, om, acc,
                l_sem, t_s, t_r, q_s, q_r, r_s, r_r, y_s, y_r, c_s, c_r):
    s, t = coords()
    n = 16
    grp = t // 2
    HD = q.shape[1]
    rows = tab.shape[0]
    heads = q.shape[0] // rows
    M = CAP * heads
    barrier = pltpu.get_barrier_semaphore()

    @pl.loop(1, n)
    def _(i):
        signal(barrier, ((s + i) % n, t))

    pool_copy = pltpu.make_async_copy(pool.at[grp], kvp, l_sem.at[0])
    arr_copy = pltpu.make_async_copy(arr.at[grp], kva, l_sem.at[1])
    pool_copy.start()
    arr_copy.start()

    i2 = lax.broadcasted_iota(jnp.int32, (n * M, 128), 0)
    slot = i2 // heads
    head = i2 % heads
    secs = [sec[e] for e in range(sec.shape[0])]
    targets = []
    for e, d in enumerate(secs):
        rank = sum([(secs[p] == d).astype(jnp.int32) for p in range(e)], jnp.int32(0))
        targets.append(d * CAP + rank)
    ids = jnp.full((n * M, 128), -1, jnp.int32)
    for e, target in enumerate(targets):
        ids = jnp.where(slot == target, row[e] * heads + head, ids)
    tb[...] = ids.reshape(n, M, 128)

    def exchange(src, dst, ss, rs, i):
        d = (s + i) % n
        return remote(src.at[d], dst.at[s], ss.at[i], rs.at[i], (d, t))

    def start_all(src, dst, ss, rs):
        @pl.loop(1, n)
        def _(i):
            exchange(src, dst, ss, rs, i).start()

    def wait_all(src, dst, ss, rs):
        @pl.loop(1, n)
        def _(i):
            exchange(src, dst, ss, rs, i).wait_recv()

    pl.semaphore_wait(barrier, n - 1)
    start_all(tb, tr, t_s, t_r)
    tr[s] = tb[s]

    pool_copy.wait()
    lane = lax.broadcasted_iota(jnp.int32, (rows, 128), 1)
    lens = tab[:, 4:5]
    ok = []
    for b in range(kvp.shape[0]):
        limit = jnp.zeros((rows, 1), jnp.int32)
        for j in range(4):
            limit = jnp.maximum(limit, jnp.where(tab[:, j:j + 1] == b, lens - j * 128, 0))
        ok.append((lane < limit).astype(F32))
    ok = jnp.concatenate(ok, axis=1)
    ok = jnp.broadcast_to(ok[:, None, :], (rows, heads, ok.shape[1])).reshape(rows * heads, -1)
    kv = kvp[...].reshape(-1, 2 * HD)

    wait_all(tb, tr, t_s, t_r)
    ids = tr[...].reshape(n * M, 128)
    lane2 = lax.broadcasted_iota(jnp.int32, (n * M, 128), 1)
    pick = jnp.concatenate([(ids == lane2 + 128 * c).astype(F32) for c in range(q.shape[0] // 128)], axis=1)
    qs[...] = jnp.dot(pick.astype(BF), q[...], preferred_element_type=F32).astype(BF).reshape(n, M, HD)
    start_all(qs, qr, q_s, q_r)
    qr[s] = qs[s]

    m_p, l_p, o_p = softmax_parts(q[...], kv[:, :HD], kv[:, HD:], ok > 0.5)
    om[...] = o_p

    arr_copy.wait()
    kv = kva[...].reshape(-1, 2 * HD)
    allowed = jnp.concatenate([(slot == target).astype(F32) for target in targets], axis=1)
    wait_all(qs, qr, q_s, q_r)
    m_n, l_n, o_n = softmax_parts(qr[...].reshape(n * M, HD), kv[:, :HD], kv[:, HD:], allowed > 0.5)
    rb[:, :M] = o_n.reshape(n, M, HD)
    rb[:, M:] = jnp.where(lane2 == 0, m_n, l_n).reshape(n, M, 128)
    start_all(rb, rr, r_s, r_r)
    rr[s] = rb[s]
    wait_all(rb, rr, r_s, r_r)

    o_n = rr[:, :M].reshape(n * M, HD)
    ml = rr[:, M:].reshape(n * M, 128)
    size = n * M
    eye = lax.broadcasted_iota(jnp.int32, (size, size), 0) == lax.broadcasted_iota(jnp.int32, (size, size), 1)
    m_row = jnp.sum(jnp.where(eye, ml[:, 0:1], 0.0), axis=0, keepdims=True)
    l_row = jnp.sum(jnp.where(eye, ml[:, 1:2], 0.0), axis=0, keepdims=True)
    id_row = jnp.sum(jnp.where(eye, ids[:, 0:1].astype(F32), 0.0), axis=0, keepdims=True)
    mine = lax.broadcasted_iota(jnp.int32, (rows * heads, size), 0).astype(F32) == id_row
    logit = jnp.where(mine, m_row, NEG_LARGE)
    top = jnp.maximum(m_p, jnp.max(logit, axis=1, keepdims=True))
    w = jnp.where(mine, jnp.exp(logit - top), 0.0)
    scale = jnp.exp(m_p - top)
    total = scale * l_p + jnp.sum(w * l_row, axis=1, keepdims=True)
    acc[...] = (scale * om[...] + jnp.dot(w.astype(BF), o_n.astype(BF), preferred_element_type=F32)) / total
    for h in range(heads):
        att[s, :, h * HD:(h + 1) * HD] = acc[pl.ds(h, rows, stride=heads), :].astype(BF)

    x, y, core = s // 8, (s // 2) % 4, s % 2
    mate = (section_of(x, y, 1 - core), t)
    xpeer = (section_of(1 - x, y, core), t)
    ways = ((section_of(x, (y + 1) % 4, core), t), (section_of(x, (y + 3) % 4, core), t))

    def ycopy(way, k, h):
        xx = x if h == 0 else 1 - x
        blk = section_of(xx, (y + (0 if k == 0 else (3 if way == 0 else 1))) % 4, core)
        return remote(att.at[blk], att.at[blk], y_s.at[way, k, h], y_r.at[way, k, h], ways[way])

    def ylast(way):
        blk = section_of(way, (y + (3 if way == 0 else 1)) % 4, core)
        return remote(att.at[blk], att.at[blk], y_s.at[way, 1, 0], y_r.at[way, 1, 0], ways[way])

    def xcopy():
        return remote(att.at[s], att.at[s], y_s.at[0, 1, 1], y_r.at[0, 1, 1], xpeer)

    def give(i, blk):
        c = remote(att.at[blk], att.at[blk], c_s.at[i], c_r.at[i], mate)
        c.start()

    xcopy().start()
    for way in (0, 1):
        ycopy(way, 0, 0).start()
    give(0, s)
    xcopy().wait_recv()
    for way in (0, 1):
        ycopy(way, 0, 1).start()
    give(1, section_of(1 - x, y, core))
    for way in (0, 1):
        for h in (0, 1):
            ycopy(way, 0, h).wait_recv()
        ylast(way).start()
        for h in (0, 1):
            xx = x if h == 0 else 1 - x
            give(2 + 2 * way + h, section_of(xx, (y + (3 if way == 0 else 1)) % 4, core))
    for way in (0, 1):
        ylast(way).wait_recv()
        give(6 + way, section_of(way, (y + 2) % 4, core))
    for i in range(8):
        c = remote(att.at[s], att.at[s], c_s.at[i], c_r.at[i], mate)
        c.wait_recv()
        c.wait_send()
    for way in (0, 1):
        for h in (0, 1):
            ycopy(way, 0, h).wait_send()
        ylast(way).wait_send()
    xcopy().wait_send()

    @pl.loop(1, n)
    def _(i):
        exchange(tb, tr, t_s, t_r, i).wait_send()
        exchange(qs, qr, q_s, q_r, i).wait_send()
        exchange(rb, rr, r_s, r_r, i).wait_send()


def attn_call(sec, row, q, tab, pool, arr):
    rows = tab.shape[0]
    n = 16
    HD = q.shape[1]
    heads = q.shape[0] // rows
    M = CAP * heads
    dma = pltpu.SemaphoreType.DMA
    vm = pl.BlockSpec(memory_space=pltpu.VMEM)
    hbm = pl.BlockSpec(memory_space=pl.ANY)
    sm = pl.BlockSpec(memory_space=pltpu.SMEM)
    return pl.pallas_call(
        attn_kernel,
        out_shape=jax.ShapeDtypeStruct((n, rows, heads * HD), BF),
        in_specs=[sm, sm, vm, vm, hbm, hbm],
        out_specs=vm,
        scratch_shapes=[
            pltpu.VMEM(pool.shape[1:], BF),
            pltpu.VMEM(arr.shape[1:], BF),
            pltpu.VMEM((n, M, 128), jnp.int32),
            pltpu.VMEM((n, M, 128), jnp.int32),
            pltpu.VMEM((n, M, HD), BF),
            pltpu.VMEM((n, M, HD), BF),
            pltpu.VMEM((n, 2 * M, HD), F32),
            pltpu.VMEM((n, 2 * M, HD), F32),
            pltpu.VMEM((rows * heads, HD), F32),
            pltpu.VMEM((rows * heads, HD), F32),
            dma((2,)), dma((n,)), dma((n,)), dma((n,)), dma((n,)), dma((n,)), dma((n,)),
            dma((2, 2, 2)), dma((2, 2, 2)), dma((8,)), dma((8,)),
        ],
        compiler_params=pltpu.CompilerParams(
            collective_id=3, has_side_effects=True, vmem_limit_bytes=VMEM_LIMIT),
        name="attention",
    )(sec, row, q, tab, pool, arr)


def body(
    queries,
    kv_pool,
    block_table,
    cached_lengths,
    arrivals,
    arrival_section,
    arrival_row,
    out_weight,
    residual,
    norm_gain,
    gate_weight,
    up_weight,
):
    rows, heads, head_dim = queries.shape
    table = jnp.concatenate([block_table, cached_lengths[:, None]], axis=1)
    att = attn_call(arrival_section, arrival_row, queries.reshape(rows * heads, head_dim), table, kv_pool, arrivals)
    attn_proj, mg, sq = proj_call(att.reshape(-1, att.shape[2]), out_weight, residual, norm_gain.reshape(1, -1))
    hidden = ffn_call(mg.reshape(-1, mg.shape[2]), gate_weight, up_weight, sq)
    return (attn_proj, hidden)


def solution(mesh):
    placed = (
        P("section", "tensor", None),
        P(None, "section", None, None),
        P("section", None),
        P("section"),
        P(None, "section", None, None),
        P("section"),
        P("section"),
        P("tensor", "section"),
        P("tensor", "section"),
        P("section"),
        P("section", "tensor"),
        P("section", "tensor"),
    )
    return jax.shard_map(
        body,
        mesh=mesh,
        in_specs=placed,
        out_specs=(P("tensor", "section"), P("section", "tensor")),
        check_vma=False,
    )
```

```python
import jax
import jax.numpy as jnp
from jax import lax
from jax.experimental import pallas as pl
from jax.experimental.pallas import tpu as pltpu
from jax.sharding import PartitionSpec as P

MESH = pl.DeviceIdType.MESH
CAP = 2
NEG_LARGE = -1e30
EPSILON = 1e-05
VMEM_LIMIT = 60 * 1024 * 1024
BF = jnp.bfloat16
F32 = jnp.float32
N = 16
CA = 512


def section_of(x, y, core):
    return x * 8 + y * 2 + core


def remote(src, dst, ssem, rsem, dev):
    return pltpu.make_async_remote_copy(
        src_ref=src, dst_ref=dst, send_sem=ssem, recv_sem=rsem,
        device_id=dev, device_id_type=MESH)


def signal(sem, dev):
    pl.semaphore_signal(sem, inc=1, device_id=dev, device_id_type=MESH)


def layer_kernel(sec, row, q, tab, lens, pool, arr, wo_in, res, gain, gate, up,
                 proj_out, hid,
                 kvp, kva, tb, tr, qs, qr, rb, rr, sp, om, acc, att, wo,
                 pz, rbuf, sbuf, xs, xr, mgf, wf,
                 pb, pa, bs, br, as_, ar, xas, xar, xbs, xbr, ps, pr, sq, sqr, fin,
                 l_sem, t_s, t_r, q_s, q_r, r_s, r_r, y_s, y_r, c_s, c_r,
                 rs_s, rs_r, px_s, px_r, ag_s, ag_r, gx_s, gx_r, mt_s, mt_r,
                 w_s, w_r, bss, brs, ass, ars, xass, xars, xbss, xbrs, pss, prs,
                 sqs, sqrs, dgs, dgr):
    s, t = lax.axis_index("section"), lax.axis_index("tensor")
    x, y, core = s // 8, (s // 2) % 4, s % 2
    xh, z = t // 8, t % 8
    diag = s == t
    off_diag = jnp.logical_not(diag)
    mate = (section_of(x, y, 1 - core), t)
    xpeer = (section_of(1 - x, y, core), t)
    hpeer = (s, (1 - xh) * 8 + z)

    def ydev(way):
        return (section_of(x, (y + 1 + 2 * way) % 4, core), t)

    def zdev(way):
        return (s, xh * 8 + (z + 1 + 6 * way) % 8)

    barrier = pltpu.get_barrier_semaphore()

    @pl.loop(1, N)
    def _(i):
        signal(barrier, ((s + i) % N, t))

    for dev in (zdev(0), zdev(1), hpeer):
        signal(barrier, dev)

    @pl.when(off_diag)
    def _():
        signal(barrier, (s, s))

    pool_copy = pltpu.make_async_copy(pool.at[t // 2], kvp, l_sem.at[0])
    arr_copy = pltpu.make_async_copy(arr.at[t // 2], kva, l_sem.at[1])
    wo_copy = pltpu.make_async_copy(wo_in, wo, l_sem.at[2])

    def w_own(c):
        return pltpu.make_async_copy(gate if c == 0 else up, wf.at[c], l_sem.at[3])

    def w_far(c):
        return remote(up if c == 0 else gate, wf.at[c], w_s, w_r, mate)

    pool_copy.start()
    arr_copy.start()
    wo_copy.start()

    HD = q.shape[1]
    rows = res.shape[0]
    heads = q.shape[0] // rows
    M = CAP * heads
    i2 = lax.broadcasted_iota(jnp.int32, (N * M, 128), 0)
    slot = i2 // heads
    head = i2 % heads
    secs = [sec[e] for e in range(sec.shape[0])]
    targets = []
    for e, d in enumerate(secs):
        rank = sum([(secs[p] == d).astype(jnp.int32) for p in range(e)], jnp.int32(0))
        targets.append(d * CAP + rank)
    ids = jnp.full((N * M, 128), -1, jnp.int32)
    for e, target in enumerate(targets):
        ids = jnp.where(slot == target, row[e] * heads + head, ids)
    tb[...] = ids.reshape(N, M, 128)

    def exchange(src, dst, ss, rs, i):
        d = (s + i) % N
        return remote(src.at[d], dst.at[s], ss.at[i], rs.at[i], (d, t))

    def start_all(src, dst, ss, rs):
        @pl.loop(1, N)
        def _(i):
            exchange(src, dst, ss, rs, i).start()

    def wait_all(src, dst, ss, rs):
        @pl.loop(1, N)
        def _(i):
            exchange(src, dst, ss, rs, i).wait_recv()

    @pl.when(diag)
    def _():
        pl.semaphore_wait(barrier, 2 * (N - 1) + 3)

    @pl.when(off_diag)
    def _():
        pl.semaphore_wait(barrier, N - 1 + 3)

    start_all(tb, tr, t_s, t_r)
    tr[s] = tb[s]
    for c in (0, 1):
        @pl.when(core == c)
        def _():
            w_own(c).start()
            w_far(c).start()

    blocks = kvp.shape[0]
    len_row = lens[...].reshape(1, rows)
    which = lax.broadcasted_iota(jnp.int32, (2 * blocks, rows), 0)
    limits = jnp.zeros((2 * blocks, rows), jnp.int32)
    for b in range(blocks):
        limit = jnp.zeros((1, rows), jnp.int32)
        for j in range(tab.shape[0]):
            limit = jnp.maximum(limit, jnp.where(tab[j:j + 1, :] == b, len_row - j * 128, 0))
        limits = jnp.where(which == b, limit // 2, jnp.where(which == blocks + b, limit % 2, limits))
    spread = (lax.broadcasted_iota(jnp.int32, (rows * heads, rows), 0) // heads
              == lax.broadcasted_iota(jnp.int32, (rows * heads, rows), 1)).astype(F32).astype(BF)
    limits = lax.dot_general(spread, limits.astype(F32).astype(BF), (((1,), (1,)), ((), ())),
                             preferred_element_type=F32)
    lane = lax.broadcasted_iota(jnp.int32, (rows * heads, 128), 1).astype(F32)
    ok = [lane < 2.0 * limits[:, b:b + 1] + limits[:, blocks + b:blocks + b + 1] for b in range(blocks)]
    pool_copy.wait()
    kv = kvp[...].reshape(-1, 2 * HD)
    scale_qk = HD ** -0.5

    def scores(a, k):
        return lax.dot_general(a, k, (((1,), (1,)), ((), ())), preferred_element_type=F32) * scale_qk

    okc = jnp.concatenate([o.astype(F32) for o in ok], axis=1) > 0.5
    sc = jnp.where(okc, scores(q[...], kv[:, :HD]), NEG_LARGE)
    m_p = jnp.max(sc, axis=1, keepdims=True)
    p = jnp.where(okc, jnp.exp(sc - m_p), 0.0)
    l_p = jnp.sum(p, axis=1, keepdims=True)
    om[...] = jnp.dot(p.astype(BF), kv[:, HD:], preferred_element_type=F32)

    wait_all(tb, tr, t_s, t_r)
    ids = tr[...].reshape(N * M, 128)
    lane2 = lax.broadcasted_iota(jnp.int32, (N * M, 128), 1)
    pick = jnp.concatenate([(ids == lane2 + 128 * c).astype(F32) for c in range(q.shape[0] // 128)], axis=1)
    qs[...] = jnp.dot(pick.astype(BF), q[...], preferred_element_type=F32).astype(BF).reshape(N, M, HD)
    start_all(qs, qr, q_s, q_r)
    qr[s] = qs[s]

    arr_copy.wait()
    kvn = kva[...].reshape(-1, 2 * HD)
    ok_n = jnp.concatenate([(slot == target).astype(F32) for target in targets], axis=1) > 0.5
    wait_all(qs, qr, q_s, q_r)
    sn = jnp.where(ok_n, scores(qr[...].reshape(N * M, HD), kvn[:, :HD]), NEG_LARGE)
    m_n = jnp.max(sn, axis=1, keepdims=True)
    pn = jnp.where(ok_n, jnp.exp(sn - m_n), 0.0)
    l_n = jnp.sum(pn, axis=1, keepdims=True)
    o_n = jnp.dot(pn.astype(BF), kvn[:, HD:], preferred_element_type=F32)
    rb[:, :M] = o_n.reshape(N, M, HD)
    rb[:, M:] = jnp.where(lane2 == 0, m_n, l_n).reshape(N, M, 128)
    start_all(rb, rr, r_s, r_r)
    rr[s] = rb[s]

    size = N * M
    eye = lax.broadcasted_iota(jnp.int32, (size, size), 0) == lax.broadcasted_iota(jnp.int32, (size, size), 1)
    id_row = jnp.sum(jnp.where(eye, ids[:, 0:1].astype(F32), 0.0), axis=0, keepdims=True)
    mine = lax.broadcasted_iota(jnp.int32, (rows * heads, size), 0).astype(F32) == id_row
    wait_all(rb, rr, r_s, r_r)
    o_n = rr[:, :M].reshape(size, HD)
    ml = rr[:, M:].reshape(size, 128)
    m_row = jnp.sum(jnp.where(eye, ml[:, 0:1], 0.0), axis=0, keepdims=True)
    l_row = jnp.sum(jnp.where(eye, ml[:, 1:2], 0.0), axis=0, keepdims=True)
    logit = jnp.where(mine, m_row, NEG_LARGE)
    top = jnp.maximum(m_p, jnp.max(logit, axis=1, keepdims=True))
    w = jnp.where(mine, jnp.exp(logit - top), 0.0)
    scale = jnp.exp(m_p - top)
    total = scale * l_p + jnp.sum(w * l_row, axis=1, keepdims=True)
    acc[...] = (scale * om[...] + jnp.dot(w.astype(BF), o_n.astype(BF), preferred_element_type=F32)) / total
    for h in range(heads):
        att[s, :, h * HD:(h + 1) * HD] = acc[pl.ds(h, rows, stride=heads), :].astype(BF)

    def ycopy(way, h):
        xx = x if h == 0 else 1 - x
        src = section_of(xx, y, core)
        return remote(att.at[src], att.at[src], y_s.at[way, 0, h], y_r.at[way, 0, h], ydev(way))

    def ylast(way):
        blk = section_of(way, (y + 3 - 2 * way) % 4, core)
        return remote(att.at[blk], att.at[blk], y_s.at[way, 1, 0], y_r.at[way, 1, 0], ydev(way))

    def xcopy():
        return remote(att.at[s], att.at[s], y_s.at[0, 1, 1], y_r.at[0, 1, 1], xpeer)

    def give(i, blk):
        remote(att.at[blk], att.at[blk], c_s.at[i], c_r.at[i], mate).start()

    xcopy().start()
    for way in (0, 1):
        ycopy(way, 0).start()
    give(0, s)
    xcopy().wait_recv()
    for way in (0, 1):
        ycopy(way, 1).start()
    give(1, section_of(1 - x, y, core))
    for way in (0, 1):
        for h in (0, 1):
            ycopy(way, h).wait_recv()
        ylast(way).start()
        for h in (0, 1):
            give(2 + 2 * way + h, section_of(x if h == 0 else 1 - x, (y + 3 - 2 * way) % 4, core))
    for way in (0, 1):
        ylast(way).wait_recv()
        give(6 + way, section_of(way, (y + 2) % 4, core))
    wo_copy.wait()
    for i in range(8):
        remote(att.at[s], att.at[s], c_s.at[i], c_r.at[i], mate).wait_recv()

    def project(slot_, off):
        zz = (z + off) % 8
        a = jnp.concatenate([att[zz], att[8 + zz]], 0)
        v = jnp.dot(a, wo[...], preferred_element_type=F32)
        pz[slot_, 0] = v[:rows]
        pz[slot_, 1] = v[rows:]

    def off_of(slot_):
        k = (slot_ + 1) // 2
        return jnp.where(slot_ % 2 == 1, 4 - k, 4 + k) % 8

    def rs(way, k, h):
        return remote(sbuf.at[way, k, h], rbuf.at[way, k, h], rs_s.at[way, k, h], rs_r.at[way, k, h], zdev(way))

    def rs_send(way, k, h, add):
        v = pz[0 if k == 0 else 2 * k - 1 + way, h]
        if add:
            rs(way, k - 1, h).wait_recv()
            v = v + rbuf[way, k - 1, h].astype(F32)
        sbuf[way, k, h] = v.astype(BF)
        rs(way, k, h).start()

    halves = (1 - xh, xh)
    project(0, 4)
    for h in halves:
        rs_send(h, 0, h, False)

    @pl.loop(1, 3)
    def _(i):
        project(i, off_of(i))

    for h in halves:
        rs_send(1 - h, 1, h, False)

    @pl.loop(3, 8)
    def _(i):
        project(i, off_of(i))

    for k in (1, 2, 3):
        for h in halves:
            rs_send(h, k, h, True)
            if k > 1:
                rs_send(1 - h, k, h, True)

    def rs_total(h):
        for way in (0, 1):
            rs(way, 3, h).wait_recv()
        return pz[7, h] + rbuf[0, 3, h].astype(F32) + rbuf[1, 3, h].astype(F32)

    def pair_copy():
        return remote(xs, xr, px_s, px_r, hpeer)

    xs[...] = rs_total(1 - xh).astype(BF)
    pair_copy().start()
    part_own = rs_total(xh)
    pair_copy().wait_recv()
    proj = part_own + xr[...].astype(F32)
    mixed = proj + res[...].astype(F32)
    mgf[core, t] = (mixed * gain[...].reshape(1, -1).astype(F32)).astype(BF)

    def agx():
        return remote(mgf.at[core, t], mgf.at[core, t], gx_s, gx_r, hpeer)

    def blk_of(way, k, r):
        return (xh if r == 0 else 1 - xh) * 8 + (z + 8 + (2 * way - 1) * k) % 8

    def ag(way, k, r):
        ref = mgf.at[core, blk_of(way, k, r)]
        return remote(ref, ref, ag_s.at[way, k, r], ag_r.at[way, k, r], zdev(way))

    def main(r):
        return xh if r == 0 else 1 - xh

    def hand(r, i, blk):
        ref = mgf.at[core, blk]
        remote(ref, ref, mt_s.at[r, i], mt_r.at[r, i], mate).start()

    def hand_wait(r):
        for i in range(8):
            ref = mgf.at[core, t]
            remote(ref, ref, mt_s.at[r, i], mt_r.at[r, i], mate).wait_recv()

    def ag_step(k, r):
        for way in (0, 1):
            ag(way, k - 1, r).wait_recv()
            if k < 3:
                ag(way, k, r).start()
        if k == 3:
            ag(main(r), 3, r).start()
        for way in (0, 1):
            hand(r, 2 * (k - 1) + 1 + way, blk_of(way, k, r))

    def ag_end(r):
        ag(main(r), 3, r).wait_recv()
        hand(r, 7, blk_of(0, 4, r))

    for way in (0, 1):
        ag(way, 0, 0).start()
    agx().start()
    hand(0, 0, t)
    proj_out[...] = proj
    sq[...] = jnp.sum(mixed * mixed, axis=1, keepdims=True) + jnp.zeros(sq.shape, F32)

    def sq_copy(i):
        return remote(sq, sqr.at[i], sqs, sqrs.at[i], (t, t))

    def dg_copy(i):
        return remote(fin, fin, dgs.at[i], dgr, (s, (t + i) % N))

    @pl.when(off_diag)
    def _():
        sq_copy((s - t + N) % N).start()

    ag_step(1, 0)
    agx().wait_recv()
    for way in (0, 1):
        ag(way, 0, 1).start()
    hand(1, 0, (1 - xh) * 8 + z)
    ag_step(2, 0)
    ag_step(1, 1)
    ag_step(3, 0)
    ag_end(0)

    R = 2 * rows
    FFN = gate.shape[1]
    CB = FFN - CA
    H = CA // 2
    for c in (0, 1):
        @pl.when(core == c)
        def _():
            w_own(c).wait()
            w_far(c).wait_recv()

    def yoff(k):
        return (y + jnp.where(k == 0, 2, jnp.where(k == 1, 1, jnp.where(k == 2, 3, 0)))) % 4

    def ffn_part(hf, pos, hx):
        k = (0, 2 - hx, 1 + hx, 3)[pos]
        b = hx * 8 + 2 * yoff(k)
        a0 = mgf[0, pl.ds(b, 2)].reshape(R, -1)
        a1 = mgf[1, pl.ds(b, 2)].reshape(R, -1)

        def cols(c0, c1):
            return (jnp.dot(a0, wf[0, :, c0:c1], preferred_element_type=F32)
                    + jnp.dot(a1, wf[1, :, c0:c1], preferred_element_type=F32))

        pb[hf, pos] = cols(CA, FFN)
        pa[hf, pos] = cols(0, CA)

        @pl.when(hx != x)
        def _():
            xas[pos] = pa[hf, pos].astype(BF)
            xacopy(pos).start()

    def bcopy(way, m):
        return remote(bs.at[way, m], br.at[way, m], bss.at[way, m], brs.at[way, m], ydev(way))

    def acopy(way, m):
        return remote(as_.at[way, m], ar.at[way, m], ass.at[way, m], ars.at[way, m], ydev(way))

    def xacopy(k):
        return remote(xas.at[k], xar.at[k], xass.at[k], xars.at[k], xpeer)

    def xbcopy():
        return remote(xbs, xbr, xbss, xbrs, xpeer)

    def ffn_half(hf, hx, between):
        hand_wait(hf)
        ffn_part(hf, 0, hx)
        bs[hx, 0] = pb[hf, 0].astype(BF)
        bcopy(hx, 0).start()
        between(0)
        ffn_part(hf, 1, hx)
        bs[1 - hx, 1] = pb[hf, 1].astype(BF)
        bcopy(1 - hx, 1).start()
        between(1)
        ffn_part(hf, 2, hx)
        between(2)
        bcopy(hx, 0).wait_recv()
        bs[hx, 2] = (pb[hf, 2] + br[hx, 0].astype(F32)).astype(BF)
        bcopy(hx, 2).start()
        ffn_part(hf, 3, hx)

    def between(i):
        if i == 0:
            ag_step(2, 1)
        elif i == 1:
            ag_step(3, 1)
        else:
            ag_end(1)

    ffn_half(0, xh, between)
    ffn_half(1, 1 - xh, lambda i: None)

    ho = jnp.where(x == xh, 0, 1)

    def a_sum(pos):
        xacopy(pos).wait_recv()
        pa[ho, pos] = pa[ho, pos] + xar[pos].astype(F32)

    def a_pos(way):
        return jnp.where(way == x, 2, 1)

    a_sum(0)
    for way in (0, 1):
        as_[way, 0] = pa[ho, 0, :, way * H:(way + 1) * H].astype(BF)
        acopy(way, 0).start()
    a_sum(1)
    a_sum(2)
    for way in (0, 1):
        as_[way, 1] = pa[ho, a_pos(way), :, (1 - way) * H:(2 - way) * H].astype(BF)
        acopy(way, 1).start()

    for way in (0, 1):
        bcopy(way, 1).wait_recv()
        bcopy(way, 2).wait_recv()
    for hf, hx in ((0, xh), (1, 1 - xh)):
        pb[hf, 3] = pb[hf, 3] + br[hx, 2].astype(F32) + br[1 - hx, 1].astype(F32)
    xbs[...] = pb[1 - ho, 3].astype(BF)
    xbcopy().start()

    for way in (0, 1):
        acopy(way, 0).wait_recv()
        as_[way, 2] = (pa[ho, a_pos(way), :, way * H:(way + 1) * H] + ar[way, 0].astype(F32)).astype(BF)
        acopy(way, 2).start()

    @pl.when(diag)
    def _():
        acc_sq = sq[...]
        for i in range(1, N):
            sq_copy(i).wait_recv()
            acc_sq = acc_sq + sqr[i]
        fin[...] = acc_sq
        for i in range(1, N):
            dg_copy(i).start()

    a_sum(3)
    for way in (0, 1):
        acopy(way, 1).wait_recv()
        acopy(way, 2).wait_recv()
    for h in (0, 1):
        pa[ho, 3, :, h * H:(h + 1) * H] = (pa[ho, 3, :, h * H:(h + 1) * H]
                                           + ar[h, 2].astype(F32) + ar[1 - h, 1].astype(F32))

    give_rows = pl.multiple_of((1 - core) * rows, rows)
    keep_rows = pl.multiple_of(core * rows, rows)

    def pcopy(i):
        c = (slice(0, CA), slice(CA, FFN))[i]
        return remote(ps.at[:, c], pr.at[:, c], pss.at[i], prs.at[i], mate)

    ps[:, :CA] = pa[ho, 3, pl.ds(give_rows, rows), :]
    pcopy(0).start()
    xbcopy().wait_recv()
    pb[ho, 3] = pb[ho, 3] + xbr[...].astype(F32)
    ps[:, CA:] = pb[ho, 3, pl.ds(give_rows, rows), :]
    pcopy(1).start()

    @pl.when(off_diag)
    def _():
        dg_copy(1).wait_recv()

    inv = lax.rsqrt(fin[:, :1] / (gate.shape[0] * N) + EPSILON)

    def finish(i, own, c0, c1):
        pcopy(i).wait_recv()
        other = pr[:, c0:c1] * inv
        own = own * inv
        g = jnp.where(core == 0, own, other)
        u = jnp.where(core == 0, other, own)
        hid[:, c0:c1] = g / (1.0 + jnp.exp(-g)) * u

    finish(0, pa[ho, 3, pl.ds(keep_rows, rows), :], 0, CA)
    finish(1, pb[ho, 3, pl.ds(keep_rows, rows), :], CA, FFN)

    @pl.loop(1, N)
    def _(i):
        exchange(tb, tr, t_s, t_r, i).wait_send()
        exchange(qs, qr, q_s, q_r, i).wait_send()
        exchange(rb, rr, r_s, r_r, i).wait_send()

    for i in range(8):
        remote(att.at[s], att.at[s], c_s.at[i], c_r.at[i], mate).wait_send()
        for r in (0, 1):
            ref = mgf.at[core, t]
            remote(ref, ref, mt_s.at[r, i], mt_r.at[r, i], mate).wait_send()
    xcopy().wait_send()
    pair_copy().wait_send()
    agx().wait_send()
    xbcopy().wait_send()
    for way in (0, 1):
        for h in (0, 1):
            ycopy(way, h).wait_send()
            rs(way, 1, h).wait_send()
            rs(way, 2, h).wait_send()
            rs(way, 3, h).wait_send()
            for k in range(3):
                ag(way, k, h).wait_send()
        ylast(way).wait_send()
        rs(way, 0, way).wait_send()
        ag(main(way), 3, way).wait_send()
        for m in range(3):
            bcopy(way, m).wait_send()
            acopy(way, m).wait_send()
    for k in range(4):
        xacopy(k).wait_send()
    for i in (0, 1):
        pcopy(i).wait_send()
    for c in (0, 1):
        @pl.when(core == c)
        def _():
            w_far(c).wait_send()

    @pl.when(diag)
    def _():
        for i in range(1, N):
            dg_copy(i).wait_send()

    @pl.when(off_diag)
    def _():
        sq_copy((s - t + N) % N).wait_send()


def body(
    queries,
    kv_pool,
    block_table,
    cached_lengths,
    arrivals,
    arrival_section,
    arrival_row,
    out_weight,
    residual,
    norm_gain,
    gate_weight,
    up_weight,
):
    rows, heads, hd = queries.shape
    width, ffn = gate_weight.shape
    m = CAP * heads
    cb = ffn - CA
    vm = pl.BlockSpec(memory_space=pltpu.VMEM)
    hbm = pl.BlockSpec(memory_space=pl.ANY)
    sm = pl.BlockSpec(memory_space=pltpu.SMEM)
    dma = pltpu.SemaphoreType.DMA

    def v(*shape, dtype=BF):
        return pltpu.VMEM(shape, dtype)

    scratch = [
        v(*kv_pool.shape[1:]), v(*arrivals.shape[1:]),
        v(N, m, 128, dtype=jnp.int32), v(N, m, 128, dtype=jnp.int32),
        v(N, m, hd), v(N, m, hd),
        v(N, 2 * m, hd, dtype=F32), v(N, 2 * m, hd, dtype=F32),
        v(rows * heads, kv_pool.shape[1] * kv_pool.shape[2], dtype=F32),
        v(rows * heads, hd, dtype=F32), v(rows * heads, hd, dtype=F32),
        v(N, rows, heads * hd), v(*out_weight.shape),
        v(8, 2, rows, width, dtype=F32), v(2, 4, 2, rows, width), v(2, 4, 2, rows, width),
        v(rows, width), v(rows, width), v(2, N, rows, width), v(2, width, ffn),
        v(2, 4, 2 * rows, cb, dtype=F32), v(2, 4, 2 * rows, CA, dtype=F32),
        v(2, 3, 2 * rows, cb), v(2, 3, 2 * rows, cb),
        v(2, 3, 2 * rows, CA // 2), v(2, 3, 2 * rows, CA // 2),
        v(4, 2 * rows, CA), v(4, 2 * rows, CA),
        v(2 * rows, cb), v(2 * rows, cb),
        v(rows, ffn, dtype=F32), v(rows, ffn, dtype=F32),
        v(rows, 128, dtype=F32), v(N, rows, 128, dtype=F32), v(rows, 128, dtype=F32),
        dma((4,)), dma((N,)), dma((N,)), dma((N,)), dma((N,)), dma((N,)), dma((N,)),
        dma((2, 2, 2)), dma((2, 2, 2)), dma((8,)), dma((8,)),
        dma((2, 4, 2)), dma((2, 4, 2)), dma, dma, dma((2, 4, 2)), dma((2, 4, 2)), dma, dma,
        dma((2, 8)), dma((2, 8)),
        dma, dma, dma((2, 3)), dma((2, 3)), dma((2, 3)), dma((2, 3)),
        dma((4,)), dma((4,)), dma, dma, dma((2,)), dma((2,)),
        dma, dma((N,)), dma((N,)), dma,
    ]
    return pl.pallas_call(
        layer_kernel,
        out_shape=(jax.ShapeDtypeStruct(residual.shape, F32), jax.ShapeDtypeStruct((rows, ffn), F32)),
        in_specs=[sm, sm, vm, vm, vm, hbm, hbm, hbm, vm, vm, hbm, hbm],
        out_specs=(vm, vm),
        scratch_shapes=scratch,
        compiler_params=pltpu.CompilerParams(
            collective_id=1, has_side_effects=True, vmem_limit_bytes=VMEM_LIMIT),
        name="layer",
    )(arrival_section, arrival_row, queries.reshape(rows * heads, hd), block_table.T, cached_lengths,
      kv_pool, arrivals, out_weight, residual, norm_gain, gate_weight, up_weight)


def solution(mesh):
    placed = (
        P("section", "tensor", None),
        P(None, "section", None, None),
        P("section", None),
        P("section"),
        P(None, "section", None, None),
        P("section"),
        P("section"),
        P("tensor", "section"),
        P("tensor", "section"),
        P("section"),
        P("section", "tensor"),
        P("section", "tensor"),
    )
    return jax.shard_map(
        body,
        mesh=mesh,
        in_specs=placed,
        out_specs=(P("tensor", "section"), P("section", "tensor")),
        check_vma=False,
    )
```

```python
import jax
import jax.numpy as jnp
from jax import lax
from jax.experimental import pallas as pl
from jax.experimental.pallas import tpu as pltpu
from jax.sharding import PartitionSpec as P

MESH = pl.DeviceIdType.MESH
CAP = 2
NEG_LARGE = -1e30
EPSILON = 1e-05
VMEM_LIMIT = 60 * 1024 * 1024
BF = jnp.bfloat16
F32 = jnp.float32
N = 16
CA = 512
PZ = (4, 2)
PP = 2
PA = 2
PB = 4
PX = 2


def section_of(x, y, core):
    return x * 8 + y * 2 + core


def remote(src, dst, ssem, rsem, dev):
    return pltpu.make_async_remote_copy(
        src_ref=src, dst_ref=dst, send_sem=ssem, recv_sem=rsem,
        device_id=dev, device_id_type=MESH)


def signal(sem, dev):
    pl.semaphore_signal(sem, inc=1, device_id=dev, device_id_type=MESH)


def layer_kernel(sec, row, q, tab, lens, pool, arr, wo_in, res, gain, gate, up,
                 proj_out, hid,
                 kvp, kva, tb, tr, qs, qr, eb, ef, acc, att, wo, dh, dl, dwh, dwl, idr,
                 pz, rbuf, sbuf, xs, xr, resx, mgf, wf,
                 pb, pa, bs, br, as_, ar, xas, xar, xbs, xbr, ps, pr, sq, sqr, fin,
                 l_sem, t_s, t_r, q_s, q_r, e_s, e_r, eg_s, eg_r, y_s, y_r, c_s, c_r,
                 rs_s, rs_r, px_s, px_r, ag_s, ag_r, rx_s, rx_r, mt_s, mt_r,
                 w_s, w_r, bss, brs, ass, ars, xass, xars, xbss, xbrs, pss, prs,
                 sqs, sqrs, dgs, dgr):
    s, t = lax.axis_index("section"), lax.axis_index("tensor")
    x, y, core = s // 8, (s // 2) % 4, s % 2
    xh, z = t // 8, t % 8
    diag = s == t
    off_diag = jnp.logical_not(diag)
    mate = (section_of(x, y, 1 - core), t)
    xpeer = (section_of(1 - x, y, core), t)
    hpeer = (s, (1 - xh) * 8 + z)

    def ydev(way):
        return (section_of(x, (y + 1 + 2 * way) % 4, core), t)

    def zdev(way):
        return (s, xh * 8 + (z + 1 + 6 * way) % 8)

    barrier = pltpu.get_barrier_semaphore()

    @pl.loop(1, N)
    def _(i):
        signal(barrier, ((s + i) % N, t))

    for dev in (zdev(0), zdev(1), hpeer):
        signal(barrier, dev)

    @pl.when(off_diag)
    def _():
        signal(barrier, (s, s))

    pool_copy = pltpu.make_async_copy(pool.at[t // 2], kvp, l_sem.at[0])
    arr_copy = pltpu.make_async_copy(arr.at[t // 2], kva, l_sem.at[1])
    wo_copy = pltpu.make_async_copy(wo_in, wo, l_sem.at[2])

    def w_own(c):
        return pltpu.make_async_copy(gate if c == 0 else up, wf.at[c], l_sem.at[3])

    def w_far(c):
        return remote(up if c == 0 else gate, wf.at[c], w_s, w_r, mate)

    pool_copy.start()
    arr_copy.start()
    wo_copy.start()

    HD = q.shape[1]
    rows = res.shape[0]
    heads = q.shape[0] // rows
    M = CAP * heads
    i2 = lax.broadcasted_iota(jnp.int32, (N * M, 128), 0)
    slot = i2 // heads
    head = i2 % heads
    secs = [sec[e] for e in range(sec.shape[0])]
    targets = []
    for e, d in enumerate(secs):
        rank = sum([(secs[p] == d).astype(jnp.int32) for p in range(e)], jnp.int32(0))
        targets.append(d * CAP + rank)
    ids = jnp.full((N * M, 128), -1, jnp.int32)
    for e, target in enumerate(targets):
        ids = jnp.where(slot == target, row[e], ids)
    tb[...] = ids.astype(F32).astype(BF).reshape(N, M, 128)

    def exchange(src, dst, ss, rs, i):
        d = (s + i) % N
        return remote(src.at[d], dst.at[s], ss.at[i], rs.at[i], (d, t))

    def start_all(src, dst, ss, rs):
        @pl.loop(1, N)
        def _(i):
            exchange(src, dst, ss, rs, i).start()

    def wait_all(src, dst, ss, rs):
        @pl.loop(1, N)
        def _(i):
            exchange(src, dst, ss, rs, i).wait_recv()

    @pl.when(diag)
    def _():
        pl.semaphore_wait(barrier, 2 * (N - 1) + 3)

    @pl.when(off_diag)
    def _():
        pl.semaphore_wait(barrier, N - 1 + 3)

    start_all(tb, tr, t_s, t_r)
    tr[s] = tb[s]

    def res_copy():
        return remote(res, resx, rx_s, rx_r, hpeer)

    res_copy().start()
    for c in (0, 1):
        @pl.when(core == c)
        def _():
            w_own(c).start()
            w_far(c).start()

    blocks = kvp.shape[0]
    len_row = lens[...].reshape(1, rows)
    which = lax.broadcasted_iota(jnp.int32, (2 * blocks, rows), 0)
    limits = jnp.zeros((2 * blocks, rows), jnp.int32)
    for b in range(blocks):
        limit = jnp.zeros((1, rows), jnp.int32)
        for j in range(tab.shape[0]):
            limit = jnp.maximum(limit, jnp.where(tab[j:j + 1, :] == b, len_row - j * 128, 0))
        limits = jnp.where(which == b, limit // 2, jnp.where(which == blocks + b, limit % 2, limits))
    def spread_of(shape, axis):
        return (lax.broadcasted_iota(jnp.int32, shape, axis) // heads
                == lax.broadcasted_iota(jnp.int32, shape, 1 - axis)).astype(F32).astype(BF)

    spread = spread_of((rows * heads, rows), 0)
    limits = lax.dot_general(spread, limits.astype(F32).astype(BF), (((1,), (1,)), ((), ())),
                             preferred_element_type=F32)
    lane = lax.broadcasted_iota(jnp.int32, (rows * heads, 128), 1).astype(F32)
    ok = [lane < 2.0 * limits[:, b:b + 1] + limits[:, blocks + b:blocks + b + 1] for b in range(blocks)]
    pool_copy.wait()
    kv = kvp[...].reshape(-1, 2 * HD)
    scale_qk = HD ** -0.5

    def scores(a, k):
        return lax.dot_general(a, k, (((1,), (1,)), ((), ())), preferred_element_type=F32) * scale_qk

    okc = jnp.concatenate([o.astype(F32) for o in ok], axis=1) > 0.5
    sc = jnp.where(okc, scores(q[...], kv[:, :HD]), NEG_LARGE)
    m_p = jnp.max(sc, axis=1, keepdims=True)
    p = jnp.where(okc, jnp.exp(sc - m_p), 0.0)
    l_p = jnp.sum(p, axis=1, keepdims=True)
    acc[...] = jnp.dot(p.astype(BF), kv[:, HD:], preferred_element_type=F32) / l_p
    for h in range(heads):
        att[s, :, h * HD:(h + 1) * HD] = acc[pl.ds(h, rows, stride=heads), :].astype(BF)

    def terms(v):
        hi = v.astype(BF).astype(F32)
        mid = (v - hi).astype(BF).astype(F32)
        return hi, mid, v - hi - mid

    lane_i = lax.broadcasted_iota(jnp.int32, (rows * heads, 128), 1)
    row_i = lax.broadcasted_iota(jnp.int32, (rows * heads, 128), 0)
    stats = jnp.zeros((rows * heads, 128), F32)
    for i, term in enumerate(terms(m_p) + terms(l_p)):
        stats = jnp.where(lane_i // heads == i, term, stats)
    stats = jnp.where(lane_i % heads == row_i % heads, stats, 0.0)
    att[s, :, heads * HD:] = jnp.dot(spread_of((rows, rows * heads), 1), stats.astype(BF),
                                     preferred_element_type=F32).astype(BF)

    def rows_of(ref, blk, pc, pieces):
        step = rows // pieces
        return ref.at[blk, pl.ds(pc * step, step)]

    def ycopy(way, h, pc):
        ref = rows_of(att, section_of(x if h == 0 else 1 - x, y, core), pc, PA)
        return remote(ref, ref, y_s.at[way, h, pc], y_r.at[way, h, pc], ydev(way))

    def ylast(way, pc):
        ref = rows_of(att, section_of(way, (y + 3 - 2 * way) % 4, core), pc, PA)
        return remote(ref, ref, y_s.at[way, 2, pc], y_r.at[way, 2, pc], ydev(way))

    def xcopy(pc):
        ref = rows_of(att, s, pc, PA)
        return remote(ref, ref, y_s.at[0, 3, pc], y_r.at[0, 3, pc], xpeer)

    def give(i, blk):
        remote(att.at[blk], att.at[blk], c_s.at[i], c_r.at[i], mate).start()

    for pc in range(PA):
        xcopy(pc).start()
        for way in (0, 1):
            ycopy(way, 0, pc).start()
    give(0, s)

    wait_all(tb, tr, t_s, t_r)
    asked = tr[...].reshape(N * M, 128).astype(F32)
    ids = jnp.where(asked < 0.0, -1.0, asked * heads + head.astype(F32))
    lane2 = lax.broadcasted_iota(jnp.int32, (N * M, 128), 1)
    pick = jnp.concatenate([(ids == (lane2 + 128 * c).astype(F32)).astype(F32) for c in range(q.shape[0] // 128)], axis=1)
    qs[...] = jnp.dot(pick.astype(BF), q[...], preferred_element_type=F32).astype(BF).reshape(N, M, HD)
    start_all(qs, qr, q_s, q_r)
    qr[s] = qs[s]

    for pc in range(PA):
        xcopy(pc).wait_recv()
        for way in (0, 1):
            ycopy(way, 1, pc).start()
        ycopy(x, 0, pc).wait_recv()
        ylast(x, pc).start()
    give(1, section_of(1 - x, y, core))

    E = len(targets)
    HE = heads * E
    arr_copy.wait()
    kvn = kva[...].reshape(-1, 2 * HD)
    slot_of = lax.broadcasted_iota(jnp.int32, (HE, N * M), 0)
    want = jnp.zeros((HE, N * M), jnp.int32)
    for e, target in enumerate(targets):
        want = jnp.where(slot_of % E == e, target * heads + slot_of // E, want)
    sel = (want == lax.broadcasted_iota(jnp.int32, (HE, N * M), 1)).astype(F32).astype(BF)
    ok_n = (lax.broadcasted_iota(jnp.int32, (HE, E * 128), 1) // 128
            == lax.broadcasted_iota(jnp.int32, (HE, E * 128), 0) % E)
    lane_e = lax.broadcasted_iota(jnp.int32, (HE, 128), 1)
    entry = lax.broadcasted_iota(jnp.int32, (HE, 128), 0) % E
    place = jnp.zeros((HE, 128), jnp.int32)
    for e in range(E):
        place = jnp.where(entry == e, jnp.where(lane_e == 6, secs[e], row[e]), place)
    wait_all(qs, qr, q_s, q_r)
    qn = jnp.dot(sel, qr[...].reshape(N * M, HD), preferred_element_type=F32).astype(BF)
    sn = jnp.where(ok_n, scores(qn, kvn[:, :HD]), NEG_LARGE)
    m_n = jnp.max(sn, axis=1, keepdims=True)
    pn = jnp.where(ok_n, jnp.exp(sn - m_n), 0.0)
    l_n = jnp.sum(pn, axis=1, keepdims=True)
    eb[s, :HE] = jnp.dot(pn.astype(BF), kvn[:, HD:], preferred_element_type=F32).astype(BF)
    tile = place.astype(F32)
    for i, term in enumerate(terms(m_n) + terms(l_n)):
        tile = jnp.where(lane_e == i, term, tile)
    eb[s, HE:] = tile.astype(BF)

    chips = N // 2
    chip = s // 2

    def ecopy(i):
        return remote(eb.at[s], eb.at[s], e_s.at[i], e_r.at[i], (((chip + i) % chips) * 2 + core, t))

    def egive(i):
        src = ((chip + chips - i) % chips) * 2 + core
        return remote(eb.at[src], eb.at[src], eg_s.at[i], eg_r.at[i], mate)

    for i in range(1, chips):
        ecopy(i).start()
    egive(0).start()

    for pc in range(PA):
        ycopy(1 - x, 0, pc).wait_recv()
    for way in (0, 1):
        give(2 + way, section_of(x, (y + 3 - 2 * way) % 4, core))
    for pc in range(PA):
        ycopy(1 - x, 1, pc).wait_recv()
        ylast(1 - x, pc).start()
    for pc in range(PA):
        ycopy(x, 1, pc).wait_recv()
    for way in (0, 1):
        give(4 + way, section_of(1 - x, (y + 3 - 2 * way) % 4, core))
    for way in (x, 1 - x):
        for pc in range(PA):
            ylast(way, pc).wait_recv()
        give(6 + way, section_of(way, (y + 2) % 4, core))
    for i in range(1, chips):
        ecopy(i).wait_recv()
        egive(i).start()
    wo_copy.wait()
    for i in range(8):
        remote(att.at[s], att.at[s], c_s.at[i], c_r.at[i], mate).wait_recv()

    def project(slot_, off):
        zz = (z + off) % 8
        a = jnp.concatenate([att[zz, :, :heads * HD], att[8 + zz, :, :heads * HD]], 0)
        v = jnp.dot(a, wo[...], preferred_element_type=F32)
        pz[slot_, 0] = v[:rows]
        pz[slot_, 1] = v[rows:]

    def off_of(slot_):
        k = (slot_ + 1) // 2
        return jnp.where(slot_ % 2 == 1, 4 - k, 4 + k) % 8

    def cut(r, pc):
        step = rows // PZ[r]
        return pl.ds(pc * step, step)

    def rs(way, k, r, pc):
        part = cut(r, pc)
        return remote(sbuf.at[way, k, r, part], rbuf.at[way, k, r, part],
                      rs_s.at[way, k, r, pc], rs_r.at[way, k, r, pc], zdev(way))

    def rs_send(way, k, r, add):
        for pc in range(PZ[r]):
            part = cut(r, pc)
            v = pz[0 if k == 0 else 2 * k - 1 + way, r, part]
            if add:
                rs(way, k - 1, r, pc).wait_recv()
                v = v + rbuf[way, k - 1, r, part].astype(F32)
            sbuf[way, k, r, part] = v.astype(BF)
            rs(way, k, r, pc).start()

    @pl.loop(0, 8)
    def _(i):
        project(i, off_of(i))

    for i in range(chips):
        egive(i).wait_recv()
    ef[...] = eb[...].astype(F32)
    NE = N * E
    eye = lax.broadcasted_iota(jnp.int32, (NE, NE), 0) == lax.broadcasted_iota(jnp.int32, (NE, NE), 1)
    before = lax.broadcasted_iota(jnp.int32, (NE, NE), 1) < lax.broadcasted_iota(jnp.int32, (NE, NE), 0)

    def across(col):
        return jnp.sum(jnp.where(eye, col, 0.0), axis=0, keepdims=True)

    def three(v, i, step):
        return v[:, i:i + 1] + v[:, i + step:i + step + 1] + v[:, i + 2 * step:i + 2 * step + 1]

    info = ef[:, pl.ds(HE, E), :].reshape(NE, 128)
    id_col = info[:, 6:7] * rows + info[:, 7:8]
    id_row = across(id_col)
    idr[...] = jnp.broadcast_to(id_row, idr.shape)
    same = id_col == id_row
    first = jnp.sum(jnp.where(jnp.logical_and(same, before), 1.0, 0.0), axis=1, keepdims=True) < 0.5
    pick_rows = (id_col == lax.broadcasted_iota(jnp.int32, (NE, N * rows), 1).astype(F32)).astype(F32).astype(BF)
    old = jnp.dot(pick_rows, att[...].reshape(N * rows, -1), preferred_element_type=F32)
    old_stats = old[:, heads * HD:]
    for h in range(heads):
        info = ef[:, pl.ds(HE + h * E, E), :].reshape(NE, 128)
        m_row = across(three(info, 0, 1))
        l_row = across(three(info, 3, 1))
        m_old = three(old_stats, h, heads)
        l_old = three(old_stats, 3 * heads + h, heads)
        logit = jnp.where(same, m_row, NEG_LARGE)
        top = jnp.maximum(m_old, jnp.max(logit, axis=1, keepdims=True))
        w = jnp.where(same, jnp.exp(logit - top), 0.0)
        kept = jnp.exp(m_old - top) * l_old
        total = kept + jnp.sum(w * l_row, axis=1, keepdims=True)
        old_h = old[:, h * HD:(h + 1) * HD]
        new = ef[:, pl.ds(h * E, E), :].reshape(NE, HD).astype(BF)
        joined = (kept * old_h + jnp.dot(w.astype(BF), new, preferred_element_type=F32)) / total
        diff = jnp.where(first, joined - old_h, 0.0)
        hi = diff.astype(BF)
        dh[:, h * HD:(h + 1) * HD] = hi
        dl[:, h * HD:(h + 1) * HD] = (diff - hi.astype(F32)).astype(BF)
    diff = (jnp.dot(dh[...], wo[...], preferred_element_type=F32)
            + jnp.dot(dl[...], wo[...], preferred_element_type=F32))
    dwh[...] = diff.astype(BF)
    dwl[...] = (diff - dwh[...].astype(F32)).astype(BF)

    def correct(slot_, off):
        zz = (z + off) % 8
        at = lax.broadcasted_iota(jnp.int32, (2 * rows, NE), 0)
        at = (at + zz * rows + jnp.where(at >= rows, 7 * rows, 0)).astype(F32)
        put = (at == idr[0:1, :]).astype(F32).astype(BF)
        v = (jnp.dot(put, dwh[...], preferred_element_type=F32)
             + jnp.dot(put, dwl[...], preferred_element_type=F32))
        pz[slot_, 0] = pz[slot_, 0] + v[:rows]
        pz[slot_, 1] = pz[slot_, 1] + v[rows:]

    correct(0, 4)
    for r in (0, 1):
        rs_send(r, 0, r, False)

    @pl.loop(1, 3)
    def _(i):
        correct(i, off_of(i))

    for r in (0, 1):
        rs_send(1 - r, 1, r, False)

    @pl.loop(3, 8)
    def _(i):
        correct(i, off_of(i))

    for k in (1, 2, 3):
        for r in (0, 1):
            rs_send(r, k, r, True)
            if k > 1:
                rs_send(1 - r, k, r, True)

    PR = rows // PP

    def pair_copy(r, pc):
        part = pl.ds(pc * PR, PR)
        return remote(xs.at[r, part], xr.at[r, part], px_s.at[r, pc], px_r.at[r, pc], hpeer)

    for r in (0, 1):
        for pc in range(PZ[r]):
            part = cut(r, pc)
            for way in (0, 1):
                rs(way, 3, r, pc).wait_recv()
            v = pz[7, r, part] + rbuf[0, 3, r, part].astype(F32) + rbuf[1, 3, r, part].astype(F32)
            pz[7, r, part] = v
            xs[r, part] = v.astype(BF)
            if (pc + 1) % (PZ[r] // PP) == 0:
                pair_copy(r, pc // (PZ[r] // PP)).start()

    def blk_of(way, k, r):
        return r * 8 + (z + 8 + (2 * way - 1) * k) % 8

    def ag(way, k, r, pc):
        ref = mgf.at[core, blk_of(way, k, r), cut(r, pc)]
        return remote(ref, ref, ag_s.at[way, k, r, pc], ag_r.at[way, k, r, pc], zdev(way))

    def hand(r, i, blk):
        ref = mgf.at[core, blk]
        remote(ref, ref, mt_s.at[r, i], mt_r.at[r, i], mate).start()

    def hand_wait(r):
        for i in range(8):
            ref = mgf.at[core, t]
            remote(ref, ref, mt_s.at[r, i], mt_r.at[r, i], mate).wait_recv()

    def ag_step(k, r):
        for pc in range(PZ[r]):
            for way in (0, 1):
                ag(way, k - 1, r, pc).wait_recv()
                if k < 3 or way == r:
                    ag(way, k, r, pc).start()
        for way in (0, 1):
            hand(r, 2 * (k - 1) + 1 + way, blk_of(way, k, r))

    def ag_end(r):
        for pc in range(PZ[r]):
            ag(r, 3, r, pc).wait_recv()
        hand(r, 7, blk_of(0, 4, r))

    def ag_begin(r):
        for pp in range(PP):
            part = pl.ds(pp * PR, PR)
            pair_copy(r, pp).wait_recv()
            proj = pz[7, r, part] + xr[r, part].astype(F32)
            mixed = proj + jnp.where(xh == r, res[part].astype(F32), resx[part].astype(F32))
            mgf[core, blk_of(0, 0, r), part] = (mixed * gain[...].reshape(1, -1).astype(F32)).astype(BF)
            for pc in range(pp * PZ[r] // PP, (pp + 1) * PZ[r] // PP):
                for way in (0, 1):
                    ag(way, 0, r, pc).start()

            @pl.when(xh == r)
            def _():
                proj_out[part] = proj
                sq[part] = jnp.sum(mixed * mixed, axis=1, keepdims=True) + jnp.zeros((PR, sq.shape[1]), F32)
        hand(r, 0, blk_of(0, 0, r))

    def sq_copy(i):
        return remote(sq, sqr.at[i], sqs, sqrs.at[i], (t, t))

    def dg_copy(i):
        return remote(fin, fin, dgs.at[i], dgr, (s, (t + i) % N))

    res_copy().wait_recv()
    ag_begin(0)
    ag_step(1, 0)
    ag_begin(1)

    @pl.when(off_diag)
    def _():
        sq_copy((s - t + N) % N).start()

    ag_step(2, 0)
    ag_step(1, 1)
    ag_step(3, 0)
    ag_step(2, 1)
    ag_end(0)

    R = 2 * rows
    FFN = gate.shape[1]
    CB = FFN - CA
    H = CA // 2
    BR = R // PB
    XR = R // PX
    for c in (0, 1):
        @pl.when(core == c)
        def _():
            w_own(c).wait()
            w_far(c).wait_recv()

    def yoff(k):
        return (y + jnp.where(k == 0, 2, jnp.where(k == 1, 1, jnp.where(k == 2, 3, 0)))) % 4

    def ffn_part(hf, pos, hx):
        k = (0, 2 - hx, 1 + hx, 3)[pos]
        b = hx * 8 + 2 * yoff(k)
        a0 = mgf[0, pl.ds(b, 2)].reshape(R, -1)
        a1 = mgf[1, pl.ds(b, 2)].reshape(R, -1)

        def cols(c0, c1):
            return (jnp.dot(a0, wf[0, :, c0:c1], preferred_element_type=F32)
                    + jnp.dot(a1, wf[1, :, c0:c1], preferred_element_type=F32))

        pb[hf, pos] = cols(CA, FFN)
        pa[hf, pos] = cols(0, CA)

        @pl.when(hx != x)
        def _():
            for pc in range(PX):
                part = pl.ds(pc * XR, XR)
                xas[pos, part] = pa[hf, pos, part].astype(BF)
                xacopy(pos, pc).start()

    def bcopy(way, m, pc):
        part = pl.ds(pc * BR, BR)
        return remote(bs.at[way, m, part], br.at[way, m, part], bss.at[way, m, pc], brs.at[way, m, pc], ydev(way))

    def acopy(way, m, pc):
        part = pl.ds(pc * XR, XR)
        return remote(as_.at[way, m, part], ar.at[way, m, part], ass.at[way, m, pc], ars.at[way, m, pc], ydev(way))

    def xacopy(k, pc):
        part = pl.ds(pc * XR, XR)
        return remote(xas.at[k, part], xar.at[k, part], xass.at[k, pc], xars.at[k, pc], xpeer)

    def xbcopy(pc):
        part = pl.ds(pl.multiple_of(pc * BR, BR), BR)
        return remote(xbs.at[part], xbr.at[part], xbss.at[pc], xbrs.at[pc], xpeer)

    def b_send(hf, pos, way, m, pieces=range(PB)):
        for pc in pieces:
            part = pl.ds(pc * BR, BR)
            v = pb[hf, pos, part]
            if m == 2:
                bcopy(way, 0, pc).wait_recv()
                v = v + br[way, 0, part].astype(F32)
            bs[way, m, part] = v.astype(BF)
            bcopy(way, m, pc).start()

    hand_wait(0)
    ffn_part(0, 0, 0)
    b_send(0, 0, 0, 0)
    ag_step(3, 1)
    ffn_part(0, 1, 0)
    b_send(0, 1, 1, 1)
    ag_end(1)
    ffn_part(0, 2, 0)
    ffn_part(0, 3, 0)
    b_send(0, 2, 0, 2, range(PB // 2))
    hand_wait(1)
    ffn_part(1, 0, 1)
    b_send(1, 0, 1, 0)
    b_send(0, 2, 0, 2, range(PB // 2, PB))
    ffn_part(1, 1, 1)
    b_send(1, 1, 0, 1)
    ffn_part(1, 2, 1)
    ffn_part(1, 3, 1)

    ho = x

    def a_sum(pos, pc):
        part = pl.ds(pc * XR, XR)
        xacopy(pos, pc).wait_recv()
        pa[ho, pos, part] = pa[ho, pos, part] + xar[pos, part].astype(F32)

    def a_pos(way):
        return jnp.where(way == x, 2, 1)

    for pc in range(PX):
        part = pl.ds(pc * XR, XR)
        a_sum(0, pc)
        for way in (0, 1):
            as_[way, 0, part] = pa[ho, 0, part, way * H:(way + 1) * H].astype(BF)
            acopy(way, 0, pc).start()
    b_send(1, 2, 1, 2)
    for pc in range(PX):
        part = pl.ds(pc * XR, XR)
        a_sum(1, pc)
        a_sum(2, pc)
        for way in (0, 1):
            as_[way, 1, part] = pa[ho, a_pos(way), part, (1 - way) * H:(2 - way) * H].astype(BF)
            acopy(way, 1, pc).start()
    def order(i):
        return (2 * (1 - core) + i) % PB if PB == 4 else i

    def b_join(hf, hx, pc):
        part = pl.ds(pl.multiple_of(pc * BR, BR), BR)
        bcopy(hx, 2, pc).wait_recv()
        bcopy(1 - hx, 1, pc).wait_recv()
        return pb[hf, 3, part] + br[hx, 2, part].astype(F32) + br[1 - hx, 1, part].astype(F32)

    for pc in range(PX):
        part = pl.ds(pc * XR, XR)
        for way in (0, 1):
            acopy(way, 0, pc).wait_recv()
            as_[way, 2, part] = (pa[ho, a_pos(way), part, way * H:(way + 1) * H]
                                 + ar[way, 0, part].astype(F32)).astype(BF)
            acopy(way, 2, pc).start()

    for i in range(PB):
        pc = order(i)
        part = pl.ds(pl.multiple_of(pc * BR, BR), BR)
        xbs[part] = b_join(1 - ho, 1 - x, pc).astype(BF)
        xbcopy(pc).start()

    @pl.when(diag)
    def _():
        acc_sq = sq[...]
        for i in range(1, N):
            sq_copy(i).wait_recv()
            acc_sq = acc_sq + sqr[i]
        fin[...] = acc_sq
        for i in range(1, N):
            dg_copy(i).start()

    for pc in range(PX):
        part = pl.ds(pc * XR, XR)
        a_sum(3, pc)
        for way in (0, 1):
            acopy(way, 1, pc).wait_recv()
            acopy(way, 2, pc).wait_recv()
        for h in (0, 1):
            pa[ho, 3, part, h * H:(h + 1) * H] = (pa[ho, 3, part, h * H:(h + 1) * H]
                                                  + ar[h, 2, part].astype(F32) + ar[1 - h, 1, part].astype(F32))

    give_rows = pl.multiple_of((1 - core) * rows, rows)
    keep_rows = pl.multiple_of(core * rows, rows)

    def pcopy(i):
        c = (slice(0, CA), slice(CA, FFN))[i]
        return remote(ps.at[:, c], pr.at[:, c], pss.at[i], prs.at[i], mate)

    ps[:, :CA] = pa[ho, 3, pl.ds(give_rows, rows), :]
    pcopy(0).start()
    for i in range(PB):
        pc = order(i)
        part = pl.ds(pl.multiple_of(pc * BR, BR), BR)
        pb[ho, 3, part] = b_join(ho, x, pc)
    for i in range(PB):
        pc = order(i)
        part = pl.ds(pl.multiple_of(pc * BR, BR), BR)
        xbcopy(pc).wait_recv()
        pb[ho, 3, part] = pb[ho, 3, part] + xbr[part].astype(F32)
        if i == PB // 2 - 1:
            ps[:, CA:] = pb[ho, 3, pl.ds(give_rows, rows), :]
            pcopy(1).start()

    @pl.when(off_diag)
    def _():
        dg_copy(1).wait_recv()

    inv = lax.rsqrt(fin[:, :1] / (gate.shape[0] * N) + EPSILON)

    def finish(i, own, c0, c1):
        pcopy(i).wait_recv()
        other = pr[:, c0:c1] * inv
        own = own * inv
        g = jnp.where(core == 0, own, other)
        u = jnp.where(core == 0, other, own)
        hid[:, c0:c1] = g / (1.0 + jnp.exp(-g)) * u

    finish(0, pa[ho, 3, pl.ds(keep_rows, rows), :], 0, CA)
    finish(1, pb[ho, 3, pl.ds(keep_rows, rows), :], CA, FFN)

    @pl.loop(1, N)
    def _(i):
        exchange(tb, tr, t_s, t_r, i).wait_send()
        exchange(qs, qr, q_s, q_r, i).wait_send()

    for i in range(8):
        remote(att.at[s], att.at[s], c_s.at[i], c_r.at[i], mate).wait_send()
        for r in (0, 1):
            ref = mgf.at[core, t]
            remote(ref, ref, mt_s.at[r, i], mt_r.at[r, i], mate).wait_send()
    res_copy().wait_send()
    for i in range(chips):
        egive(i).wait_send()
        if i:
            ecopy(i).wait_send()
    for pc in range(PA):
        xcopy(pc).wait_send()
        for way in (0, 1):
            ycopy(way, 0, pc).wait_send()
            ycopy(way, 1, pc).wait_send()
            ylast(way, pc).wait_send()
    for way in (0, 1):
        for pc in range(PP):
            pair_copy(way, pc).wait_send()
        for r in (0, 1):
            for pc in range(PZ[r]):
                for k in range(4):
                    if k > 0 or way == r:
                        rs(way, k, r, pc).wait_send()
                    if k < 3 or way == r:
                        ag(way, k, r, pc).wait_send()
        for m in range(3):
            for pc in range(PB):
                bcopy(way, m, pc).wait_send()
            for pc in range(PX):
                acopy(way, m, pc).wait_send()
    for pc in range(PB):
        xbcopy(pc).wait_send()
    for k in range(4):
        for pc in range(PX):
            xacopy(k, pc).wait_send()
    for i in (0, 1):
        pcopy(i).wait_send()
    for c in (0, 1):
        @pl.when(core == c)
        def _():
            w_far(c).wait_send()

    @pl.when(diag)
    def _():
        for i in range(1, N):
            dg_copy(i).wait_send()

    @pl.when(off_diag)
    def _():
        sq_copy((s - t + N) % N).wait_send()


def body(
    queries,
    kv_pool,
    block_table,
    cached_lengths,
    arrivals,
    arrival_section,
    arrival_row,
    out_weight,
    residual,
    norm_gain,
    gate_weight,
    up_weight,
):
    rows, heads, hd = queries.shape
    width, ffn = gate_weight.shape
    m = CAP * heads
    entries = arrival_section.shape[0]
    cb = ffn - CA
    vm = pl.BlockSpec(memory_space=pltpu.VMEM)
    hbm = pl.BlockSpec(memory_space=pl.ANY)
    sm = pl.BlockSpec(memory_space=pltpu.SMEM)
    dma = pltpu.SemaphoreType.DMA

    def v(*shape, dtype=BF):
        return pltpu.VMEM(shape, dtype)

    scratch = [
        v(*kv_pool.shape[1:]), v(*arrivals.shape[1:]),
        v(N, m, 128), v(N, m, 128),
        v(N, m, hd), v(N, m, hd),
        v(N, 2 * heads * entries, hd), v(N, 2 * heads * entries, hd, dtype=F32),
        v(rows * heads, hd, dtype=F32),
        v(N, rows, heads * hd + 128), v(*out_weight.shape),
        v(N * entries, heads * hd), v(N * entries, heads * hd),
        v(N * entries, width), v(N * entries, width), v(8, N * entries, dtype=F32),
        v(8, 2, rows, width, dtype=F32), v(2, 4, 2, rows, width), v(2, 4, 2, rows, width),
        v(2, rows, width), v(2, rows, width), v(rows, width), v(2, N, rows, width), v(2, width, ffn),
        v(2, 4, 2 * rows, cb, dtype=F32), v(2, 4, 2 * rows, CA, dtype=F32),
        v(2, 3, 2 * rows, cb), v(2, 3, 2 * rows, cb),
        v(2, 3, 2 * rows, CA // 2), v(2, 3, 2 * rows, CA // 2),
        v(4, 2 * rows, CA), v(4, 2 * rows, CA),
        v(2 * rows, cb), v(2 * rows, cb),
        v(rows, ffn, dtype=F32), v(rows, ffn, dtype=F32),
        v(rows, 128, dtype=F32), v(N, rows, 128, dtype=F32), v(rows, 128, dtype=F32),
        dma((4,)), dma((N,)), dma((N,)), dma((N,)), dma((N,)),
        dma((N // 2,)), dma((N // 2,)), dma((N // 2,)), dma((N // 2,)),
        dma((2, 4, PA)), dma((2, 4, PA)), dma((8,)), dma((8,)),
        dma((2, 4, 2, 4)), dma((2, 4, 2, 4)), dma((2, PP)), dma((2, PP)), dma((2, 4, 2, 4)), dma((2, 4, 2, 4)), dma, dma,
        dma((2, 8)), dma((2, 8)),
        dma, dma, dma((2, 3, PB)), dma((2, 3, PB)), dma((2, 3, PX)), dma((2, 3, PX)),
        dma((4, PX)), dma((4, PX)), dma((PB,)), dma((PB,)), dma((2,)), dma((2,)),
        dma, dma((N,)), dma((N,)), dma,
    ]
    return pl.pallas_call(
        layer_kernel,
        out_shape=(jax.ShapeDtypeStruct(residual.shape, F32), jax.ShapeDtypeStruct((rows, ffn), F32)),
        in_specs=[sm, sm, vm, vm, vm, hbm, hbm, hbm, vm, vm, hbm, hbm],
        out_specs=(vm, vm),
        scratch_shapes=scratch,
        compiler_params=pltpu.CompilerParams(
            collective_id=1, has_side_effects=True, vmem_limit_bytes=VMEM_LIMIT),
        name="layer",
    )(arrival_section, arrival_row, queries.reshape(rows * heads, hd), block_table.T, cached_lengths,
      kv_pool, arrivals, out_weight, residual, norm_gain, gate_weight, up_weight)


def solution(mesh):
    placed = (
        P("section", "tensor", None),
        P(None, "section", None, None),
        P("section", None),
        P("section"),
        P(None, "section", None, None),
        P("section"),
        P("section"),
        P("tensor", "section"),
        P("tensor", "section"),
        P("section"),
        P("section", "tensor"),
        P("section", "tensor"),
    )
    return jax.shard_map(
        body,
        mesh=mesh,
        in_specs=placed,
        out_specs=(P("tensor", "section"), P("section", "tensor")),
        check_vma=False,
    )
```

```python
import jax
import jax.numpy as jnp
from jax import lax
from jax.experimental import pallas as pl
from jax.experimental.pallas import tpu as pltpu
from jax.sharding import PartitionSpec as P

MESH = pl.DeviceIdType.MESH
CAP = 2
NEG_LARGE = -1e30
EPSILON = 1e-05
VMEM_LIMIT = 60 * 1024 * 1024
BF = jnp.bfloat16
F32 = jnp.float32
N = 16
CA = 768
PZ = (4, 2)
PP = 2
PA = 2
PB = 4
PX = 2


def section_of(x, y, core):
    return x * 8 + y * 2 + core


def remote(src, dst, ssem, rsem, dev):
    return pltpu.make_async_remote_copy(
        src_ref=src, dst_ref=dst, send_sem=ssem, recv_sem=rsem,
        device_id=dev, device_id_type=MESH)


def signal(sem, dev):
    pl.semaphore_signal(sem, inc=1, device_id=dev, device_id_type=MESH)


def layer_kernel(sec, row, q, tab, lens, pool, arr, wo_in, res, gain, gate, up,
                 proj_out, hid,
                 kvp, kva, tb, tr, qs, qr, eb, ef, acc, att, wo, dh, dl, dwh, dwl, idr,
                 pz, rbuf, sbuf, xs, xr, resx, mgf, wf,
                 pb, pa, bs, br, as_, ar, xas, xar, xbs, xbr, ps, pr, sq, sqr, fin,
                 l_sem, t_s, t_r, q_s, q_r, e_s, e_r, eg_s, eg_r, y_s, y_r, c_s, c_r,
                 rs_s, rs_r, px_s, px_r, ag_s, ag_r, rx_s, rx_r, mt_s, mt_r,
                 w_s, w_r, bss, brs, ass, ars, xass, xars, xbss, xbrs, pss, prs,
                 sqs, sqrs, dgs, dgr):
    s, t = lax.axis_index("section"), lax.axis_index("tensor")
    x, y, core = s // 8, (s // 2) % 4, s % 2
    xh, z = t // 8, t % 8
    diag = s == t
    off_diag = jnp.logical_not(diag)
    mate = (section_of(x, y, 1 - core), t)
    xpeer = (section_of(1 - x, y, core), t)
    hpeer = (s, (1 - xh) * 8 + z)

    def ydev(way):
        return (section_of(x, (y + 1 + 2 * way) % 4, core), t)

    def zdev(way):
        return (s, xh * 8 + (z + 1 + 6 * way) % 8)

    barrier = pltpu.get_barrier_semaphore()

    @pl.loop(1, N)
    def _(i):
        signal(barrier, ((s + i) % N, t))

    for dev in (zdev(0), zdev(1), hpeer):
        signal(barrier, dev)

    pool_copy = pltpu.make_async_copy(pool.at[t // 2], kvp, l_sem.at[0])
    arr_copy = pltpu.make_async_copy(arr.at[t // 2], kva, l_sem.at[1])
    wo_copy = pltpu.make_async_copy(wo_in, wo, l_sem.at[2])

    def w_own(c):
        return pltpu.make_async_copy(gate if c == 0 else up, wf.at[c], l_sem.at[3])

    def w_far(c):
        return remote(up if c == 0 else gate, wf.at[c], w_s, w_r, mate)

    pool_copy.start()
    arr_copy.start()
    wo_copy.start()

    HD = q.shape[1]
    rows = res.shape[0]
    heads = q.shape[0] // rows
    M = CAP * heads
    i2 = lax.broadcasted_iota(jnp.int32, (N * M, 128), 0)
    slot = i2 // heads
    head = i2 % heads
    secs = [sec[e] for e in range(sec.shape[0])]
    targets = []
    for e, d in enumerate(secs):
        rank = sum([(secs[p] == d).astype(jnp.int32) for p in range(e)], jnp.int32(0))
        targets.append(d * CAP + rank)
    ids = jnp.full((N * M, 128), -1, jnp.int32)
    for e, target in enumerate(targets):
        ids = jnp.where(slot == target, row[e], ids)
    tb[...] = ids.astype(F32).astype(BF).reshape(N, M, 128)

    def exchange(src, dst, ss, rs, i):
        d = (s + i) % N
        return remote(src.at[d], dst.at[s], ss.at[i], rs.at[i], (d, t))

    def start_all(src, dst, ss, rs):
        @pl.loop(1, N)
        def _(i):
            exchange(src, dst, ss, rs, i).start()

    def wait_all(src, dst, ss, rs):
        @pl.loop(1, N)
        def _(i):
            exchange(src, dst, ss, rs, i).wait_recv()

    pl.semaphore_wait(barrier, N - 1 + 3)

    start_all(tb, tr, t_s, t_r)
    tr[s] = tb[s]

    def res_copy():
        return remote(res, resx, rx_s, rx_r, hpeer)

    res_copy().start()
    for c in (0, 1):
        @pl.when(core == c)
        def _():
            w_own(c).start()
            w_far(c).start()

    blocks = kvp.shape[0]
    len_row = lens[...].reshape(1, rows)
    which = lax.broadcasted_iota(jnp.int32, (2 * blocks, rows), 0)
    limits = jnp.zeros((2 * blocks, rows), jnp.int32)
    for b in range(blocks):
        limit = jnp.zeros((1, rows), jnp.int32)
        for j in range(tab.shape[0]):
            limit = jnp.maximum(limit, jnp.where(tab[j:j + 1, :] == b, len_row - j * 128, 0))
        limits = jnp.where(which == b, limit // 2, jnp.where(which == blocks + b, limit % 2, limits))
    def spread_of(shape, axis):
        return (lax.broadcasted_iota(jnp.int32, shape, axis) // heads
                == lax.broadcasted_iota(jnp.int32, shape, 1 - axis)).astype(F32).astype(BF)

    spread = spread_of((rows * heads, rows), 0)
    limits = lax.dot_general(spread, limits.astype(F32).astype(BF), (((1,), (1,)), ((), ())),
                             preferred_element_type=F32)
    lane = lax.broadcasted_iota(jnp.int32, (rows * heads, 128), 1).astype(F32)
    ok = [lane < 2.0 * limits[:, b:b + 1] + limits[:, blocks + b:blocks + b + 1] for b in range(blocks)]
    pool_copy.wait()
    kv = kvp[...].reshape(-1, 2 * HD)
    scale_qk = HD ** -0.5

    def scores(a, k):
        return lax.dot_general(a, k, (((1,), (1,)), ((), ())), preferred_element_type=F32) * scale_qk

    okc = jnp.concatenate([o.astype(F32) for o in ok], axis=1) > 0.5
    sc = jnp.where(okc, scores(q[...], kv[:, :HD]), NEG_LARGE)
    m_p = jnp.max(sc, axis=1, keepdims=True)
    p = jnp.where(okc, jnp.exp(sc - m_p), 0.0)
    l_p = jnp.sum(p, axis=1, keepdims=True)
    acc[...] = jnp.dot(p.astype(BF), kv[:, HD:], preferred_element_type=F32) / l_p
    for h in range(heads):
        att[s, :, h * HD:(h + 1) * HD] = acc[pl.ds(h, rows, stride=heads), :].astype(BF)

    def terms(v):
        hi = v.astype(BF).astype(F32)
        mid = (v - hi).astype(BF).astype(F32)
        return hi, mid, v - hi - mid

    lane_i = lax.broadcasted_iota(jnp.int32, (rows * heads, 128), 1)
    row_i = lax.broadcasted_iota(jnp.int32, (rows * heads, 128), 0)
    stats = jnp.zeros((rows * heads, 128), F32)
    for i, term in enumerate(terms(m_p) + terms(l_p)):
        stats = jnp.where(lane_i // heads == i, term, stats)
    stats = jnp.where(lane_i % heads == row_i % heads, stats, 0.0)
    att[s, :, heads * HD:] = jnp.dot(spread_of((rows, rows * heads), 1), stats.astype(BF),
                                     preferred_element_type=F32).astype(BF)

    def rows_of(ref, blk, pc, pieces):
        step = rows // pieces
        return ref.at[blk, pl.ds(pc * step, step)]

    def ycopy(way, h, pc):
        ref = rows_of(att, section_of(x if h == 0 else 1 - x, y, core), pc, PA)
        return remote(ref, ref, y_s.at[way, h, pc], y_r.at[way, h, pc], ydev(way))

    def ylast(way, pc):
        ref = rows_of(att, section_of(way, (y + 3 - 2 * way) % 4, core), pc, PA)
        return remote(ref, ref, y_s.at[way, 2, pc], y_r.at[way, 2, pc], ydev(way))

    def xcopy(pc):
        ref = rows_of(att, s, pc, PA)
        return remote(ref, ref, y_s.at[0, 3, pc], y_r.at[0, 3, pc], xpeer)

    def give(i, blk):
        remote(att.at[blk], att.at[blk], c_s.at[i], c_r.at[i], mate).start()

    for pc in range(PA):
        xcopy(pc).start()
        for way in (0, 1):
            ycopy(way, 0, pc).start()
    give(0, s)

    wait_all(tb, tr, t_s, t_r)
    asked = tr[...].reshape(N * M, 128).astype(F32)
    ids = jnp.where(asked < 0.0, -1.0, asked * heads + head.astype(F32))
    lane2 = lax.broadcasted_iota(jnp.int32, (N * M, 128), 1)
    pick = jnp.concatenate([(ids == (lane2 + 128 * c).astype(F32)).astype(F32) for c in range(q.shape[0] // 128)], axis=1)
    qs[...] = jnp.dot(pick.astype(BF), q[...], preferred_element_type=F32).astype(BF).reshape(N, M, HD)
    start_all(qs, qr, q_s, q_r)
    qr[s] = qs[s]

    for pc in range(PA):
        xcopy(pc).wait_recv()
        for way in (0, 1):
            ycopy(way, 1, pc).start()
        ycopy(x, 0, pc).wait_recv()
        ylast(x, pc).start()
    give(1, section_of(1 - x, y, core))

    E = len(targets)
    HE = heads * E
    arr_copy.wait()
    kvn = kva[...].reshape(-1, 2 * HD)
    slot_of = lax.broadcasted_iota(jnp.int32, (HE, N * M), 0)
    want = jnp.zeros((HE, N * M), jnp.int32)
    for e, target in enumerate(targets):
        want = jnp.where(slot_of % E == e, target * heads + slot_of // E, want)
    sel = (want == lax.broadcasted_iota(jnp.int32, (HE, N * M), 1)).astype(F32).astype(BF)
    ok_n = (lax.broadcasted_iota(jnp.int32, (HE, E * 128), 1) // 128
            == lax.broadcasted_iota(jnp.int32, (HE, E * 128), 0) % E)
    lane_e = lax.broadcasted_iota(jnp.int32, (HE, 128), 1)
    entry = lax.broadcasted_iota(jnp.int32, (HE, 128), 0) % E
    place = jnp.zeros((HE, 128), jnp.int32)
    for e in range(E):
        place = jnp.where(entry == e, jnp.where(lane_e == 6, secs[e], row[e]), place)
    wait_all(qs, qr, q_s, q_r)
    qn = jnp.dot(sel, qr[...].reshape(N * M, HD), preferred_element_type=F32).astype(BF)
    sn = jnp.where(ok_n, scores(qn, kvn[:, :HD]), NEG_LARGE)
    m_n = jnp.max(sn, axis=1, keepdims=True)
    pn = jnp.where(ok_n, jnp.exp(sn - m_n), 0.0)
    l_n = jnp.sum(pn, axis=1, keepdims=True)
    eb[s, :HE] = jnp.dot(pn.astype(BF), kvn[:, HD:], preferred_element_type=F32).astype(BF)
    tile = place.astype(F32)
    for i, term in enumerate(terms(m_n) + terms(l_n)):
        tile = jnp.where(lane_e == i, term, tile)
    eb[s, HE:] = tile.astype(BF)

    chips = N // 2
    chip = s // 2

    def ecopy(i):
        return remote(eb.at[s], eb.at[s], e_s.at[i], e_r.at[i], (((chip + i) % chips) * 2 + core, t))

    def egive(i):
        src = ((chip + chips - i) % chips) * 2 + core
        return remote(eb.at[src], eb.at[src], eg_s.at[i], eg_r.at[i], mate)

    for i in range(1, chips):
        ecopy(i).start()
    egive(0).start()

    for pc in range(PA):
        ycopy(1 - x, 0, pc).wait_recv()
    for way in (0, 1):
        give(2 + way, section_of(x, (y + 3 - 2 * way) % 4, core))
    for pc in range(PA):
        ycopy(1 - x, 1, pc).wait_recv()
        ylast(1 - x, pc).start()
    for pc in range(PA):
        ycopy(x, 1, pc).wait_recv()
    for way in (0, 1):
        give(4 + way, section_of(1 - x, (y + 3 - 2 * way) % 4, core))
    for way in (x, 1 - x):
        for pc in range(PA):
            ylast(way, pc).wait_recv()
        give(6 + way, section_of(way, (y + 2) % 4, core))
    for i in range(1, chips):
        ecopy(i).wait_recv()
        egive(i).start()
    wo_copy.wait()
    for i in range(8):
        remote(att.at[s], att.at[s], c_s.at[i], c_r.at[i], mate).wait_recv()

    def project(slot_, off):
        zz = (z + off) % 8
        a = jnp.concatenate([att[zz, :, :heads * HD], att[8 + zz, :, :heads * HD]], 0)
        v = jnp.dot(a, wo[...], preferred_element_type=F32)
        pz[slot_, 0] = v[:rows]
        pz[slot_, 1] = v[rows:]

    def off_of(slot_):
        k = (slot_ + 1) // 2
        return jnp.where(slot_ % 2 == 1, 4 - k, 4 + k) % 8

    def cut(r, pc):
        step = rows // PZ[r]
        return pl.ds(pc * step, step)

    def rs(way, k, r, pc):
        part = cut(r, pc)
        return remote(sbuf.at[way, k, r, part], rbuf.at[way, k, r, part],
                      rs_s.at[way, k, r, pc], rs_r.at[way, k, r, pc], zdev(way))

    def rs_send(way, k, r, add):
        for pc in range(PZ[r]):
            part = cut(r, pc)
            v = pz[0 if k == 0 else 2 * k - 1 + way, r, part]
            if add:
                rs(way, k - 1, r, pc).wait_recv()
                v = v + rbuf[way, k - 1, r, part].astype(F32)
            sbuf[way, k, r, part] = v.astype(BF)
            rs(way, k, r, pc).start()

    @pl.loop(0, 8)
    def _(i):
        project(i, off_of(i))

    for i in range(chips):
        egive(i).wait_recv()
    ef[...] = eb[...].astype(F32)
    NE = N * E
    eye = lax.broadcasted_iota(jnp.int32, (NE, NE), 0) == lax.broadcasted_iota(jnp.int32, (NE, NE), 1)
    before = lax.broadcasted_iota(jnp.int32, (NE, NE), 1) < lax.broadcasted_iota(jnp.int32, (NE, NE), 0)

    def across(col):
        return jnp.sum(jnp.where(eye, col, 0.0), axis=0, keepdims=True)

    def three(v, i, step):
        return v[:, i:i + 1] + v[:, i + step:i + step + 1] + v[:, i + 2 * step:i + 2 * step + 1]

    info = ef[:, pl.ds(HE, E), :].reshape(NE, 128)
    id_col = info[:, 6:7] * rows + info[:, 7:8]
    id_row = across(id_col)
    idr[...] = jnp.broadcast_to(id_row, idr.shape)
    same = id_col == id_row
    first = jnp.sum(jnp.where(jnp.logical_and(same, before), 1.0, 0.0), axis=1, keepdims=True) < 0.5
    pick_rows = (id_col == lax.broadcasted_iota(jnp.int32, (NE, N * rows), 1).astype(F32)).astype(F32).astype(BF)
    old = jnp.dot(pick_rows, att[...].reshape(N * rows, -1), preferred_element_type=F32)
    old_stats = old[:, heads * HD:]
    for h in range(heads):
        info = ef[:, pl.ds(HE + h * E, E), :].reshape(NE, 128)
        m_row = across(three(info, 0, 1))
        l_row = across(three(info, 3, 1))
        m_old = three(old_stats, h, heads)
        l_old = three(old_stats, 3 * heads + h, heads)
        logit = jnp.where(same, m_row, NEG_LARGE)
        top = jnp.maximum(m_old, jnp.max(logit, axis=1, keepdims=True))
        w = jnp.where(same, jnp.exp(logit - top), 0.0)
        kept = jnp.exp(m_old - top) * l_old
        total = kept + jnp.sum(w * l_row, axis=1, keepdims=True)
        old_h = old[:, h * HD:(h + 1) * HD]
        new = ef[:, pl.ds(h * E, E), :].reshape(NE, HD).astype(BF)
        joined = (kept * old_h + jnp.dot(w.astype(BF), new, preferred_element_type=F32)) / total
        diff = jnp.where(first, joined - old_h, 0.0)
        hi = diff.astype(BF)
        dh[:, h * HD:(h + 1) * HD] = hi
        dl[:, h * HD:(h + 1) * HD] = (diff - hi.astype(F32)).astype(BF)
    diff = (jnp.dot(dh[...], wo[...], preferred_element_type=F32)
            + jnp.dot(dl[...], wo[...], preferred_element_type=F32))
    dwh[...] = diff.astype(BF)
    dwl[...] = (diff - dwh[...].astype(F32)).astype(BF)

    def correct(slot_, off):
        zz = (z + off) % 8
        at = lax.broadcasted_iota(jnp.int32, (2 * rows, NE), 0)
        at = (at + zz * rows + jnp.where(at >= rows, 7 * rows, 0)).astype(F32)
        put = (at == idr[0:1, :]).astype(F32).astype(BF)
        v = (jnp.dot(put, dwh[...], preferred_element_type=F32)
             + jnp.dot(put, dwl[...], preferred_element_type=F32))
        pz[slot_, 0] = pz[slot_, 0] + v[:rows]
        pz[slot_, 1] = pz[slot_, 1] + v[rows:]

    correct(0, 4)
    for r in (0, 1):
        rs_send(r, 0, r, False)

    @pl.loop(1, 3)
    def _(i):
        correct(i, off_of(i))

    for r in (0, 1):
        rs_send(1 - r, 1, r, False)

    @pl.loop(3, 8)
    def _(i):
        correct(i, off_of(i))

    for k in (1, 2, 3):
        for r in (0, 1):
            rs_send(r, k, r, True)
            if k > 1:
                rs_send(1 - r, k, r, True)

    PR = rows // PP

    def pair_copy(r, pc):
        part = pl.ds(pc * PR, PR)
        return remote(xs.at[r, part], xr.at[r, part], px_s.at[r, pc], px_r.at[r, pc], hpeer)

    for r in (0, 1):
        for pc in range(PZ[r]):
            part = cut(r, pc)
            for way in (0, 1):
                rs(way, 3, r, pc).wait_recv()
            v = pz[7, r, part] + rbuf[0, 3, r, part].astype(F32) + rbuf[1, 3, r, part].astype(F32)
            pz[7, r, part] = v
            xs[r, part] = v.astype(BF)
            if (pc + 1) % (PZ[r] // PP) == 0:
                pair_copy(r, pc // (PZ[r] // PP)).start()

    def blk_of(way, k, r):
        return r * 8 + (z + 8 + (2 * way - 1) * k) % 8

    def ag(way, k, r, pc):
        ref = mgf.at[core, blk_of(way, k, r), cut(r, pc)]
        return remote(ref, ref, ag_s.at[way, k, r, pc], ag_r.at[way, k, r, pc], zdev(way))

    def hand(r, i, blk):
        ref = mgf.at[core, blk]
        remote(ref, ref, mt_s.at[r, i], mt_r.at[r, i], mate).start()

    def hand_wait(r):
        for i in range(8):
            ref = mgf.at[core, t]
            remote(ref, ref, mt_s.at[r, i], mt_r.at[r, i], mate).wait_recv()

    def ag_step(k, r):
        for pc in range(PZ[r]):
            for way in (0, 1):
                ag(way, k - 1, r, pc).wait_recv()
                if k < 3 or way == r:
                    ag(way, k, r, pc).start()
        for way in (0, 1):
            hand(r, 2 * (k - 1) + 1 + way, blk_of(way, k, r))

    def ag_end(r):
        for pc in range(PZ[r]):
            ag(r, 3, r, pc).wait_recv()
        hand(r, 7, blk_of(0, 4, r))

    def ag_begin(r):
        for pp in range(PP):
            part = pl.ds(pp * PR, PR)
            pair_copy(r, pp).wait_recv()
            proj = pz[7, r, part] + xr[r, part].astype(F32)
            mixed = proj + jnp.where(xh == r, res[part].astype(F32), resx[part].astype(F32))
            mgf[core, blk_of(0, 0, r), part] = (mixed * gain[...].reshape(1, -1).astype(F32)).astype(BF)
            for pc in range(pp * PZ[r] // PP, (pp + 1) * PZ[r] // PP):
                for way in (0, 1):
                    ag(way, 0, r, pc).start()

            @pl.when(xh == r)
            def _():
                proj_out[part] = proj
                sq[part] = jnp.sum(mixed * mixed, axis=1, keepdims=True) + jnp.zeros((PR, sq.shape[1]), F32)
        hand(r, 0, blk_of(0, 0, r))

    def sq_copy(i):
        return remote(sq, sqr.at[i], sqs, sqrs.at[i], (t, t))

    def fin_copy(way):
        return remote(fin, fin, dgs.at[way], dgr, zdev(way))

    def fin_pair():
        return remote(fin, fin, dgs.at[2], dgr, hpeer)

    dz = (z + 8 - s % 8) % 8
    hops = jnp.where(dz <= 4, dz, 8 - dz) + jnp.where(xh == s // 8, 0, 1)
    on_right = dz <= 3
    on_left = jnp.logical_or(dz == 0, dz >= 6)

    def spread_step(p):
        @pl.when(hops == p)
        def _():
            if p == 0:
                total_sq = sq[...]
                for i in range(1, N):
                    sq_copy(i).wait_recv()
                    total_sq = total_sq + sqr[i]
                fin[...] = total_sq
                fin_pair().start()
            else:
                fin_copy(0).wait_recv()

            @pl.when(on_right)
            def _():
                fin_copy(0).start()

            @pl.when(on_left)
            def _():
                fin_copy(1).start()

    res_copy().wait_recv()
    ag_begin(0)
    ag_step(1, 0)
    ag_begin(1)

    @pl.when(off_diag)
    def _():
        sq_copy((s - t + N) % N).start()

    ag_step(2, 0)
    ag_step(1, 1)
    ag_step(3, 0)
    ag_step(2, 1)
    ag_end(0)
    spread_step(0)

    R = 2 * rows
    FFN = gate.shape[1]
    CB = FFN - CA
    H = CA // 2
    BR = R // PB
    XR = R // PX
    for c in (0, 1):
        @pl.when(core == c)
        def _():
            w_own(c).wait()
            w_far(c).wait_recv()

    def yoff(k):
        return (y + jnp.where(k == 0, 2, jnp.where(k == 1, 1, jnp.where(k == 2, 3, 0)))) % 4

    def ffn_part(hf, pos, hx):
        k = (0, 2 - hx, 1 + hx, 3)[pos]
        b = hx * 8 + 2 * yoff(k)
        a0 = mgf[0, pl.ds(b, 2)].reshape(R, -1)
        a1 = mgf[1, pl.ds(b, 2)].reshape(R, -1)

        def cols(c0, c1):
            return (jnp.dot(a0, wf[0, :, c0:c1], preferred_element_type=F32)
                    + jnp.dot(a1, wf[1, :, c0:c1], preferred_element_type=F32))

        pb[hf, pos] = cols(CA, FFN)
        pa[hf, pos] = cols(0, CA)

        @pl.when(hx != x)
        def _():
            for pc in range(PX):
                part = pl.ds(pc * XR, XR)
                xas[pos, part] = pa[hf, pos, part].astype(BF)
                xacopy(pos, pc).start()

    def bcopy(way, m, pc):
        part = pl.ds(pc * BR, BR)
        return remote(bs.at[way, m, part], br.at[way, m, part], bss.at[way, m, pc], brs.at[way, m, pc], ydev(way))

    def acopy(way, m, pc):
        part = pl.ds(pc * XR, XR)
        return remote(as_.at[way, m, part], ar.at[way, m, part], ass.at[way, m, pc], ars.at[way, m, pc], ydev(way))

    def xacopy(k, pc):
        part = pl.ds(pc * XR, XR)
        return remote(xas.at[k, part], xar.at[k, part], xass.at[k, pc], xars.at[k, pc], xpeer)

    def xbcopy(pc):
        part = pl.ds(pl.multiple_of(pc * BR, BR), BR)
        return remote(xbs.at[part], xbr.at[part], xbss.at[pc], xbrs.at[pc], xpeer)

    def b_send(hf, pos, way, m, pieces=range(PB)):
        for pc in pieces:
            part = pl.ds(pc * BR, BR)
            v = pb[hf, pos, part]
            if m == 2:
                bcopy(way, 0, pc).wait_recv()
                v = v + br[way, 0, part].astype(F32)
            bs[way, m, part] = v.astype(BF)
            bcopy(way, m, pc).start()

    hand_wait(0)
    ffn_part(0, 0, 0)
    b_send(0, 0, 0, 0)
    ag_step(3, 1)
    ffn_part(0, 1, 0)
    b_send(0, 1, 1, 1)
    spread_step(1)
    ag_end(1)
    ffn_part(0, 2, 0)
    ffn_part(0, 3, 0)
    b_send(0, 2, 0, 2, range(PB // 2))
    spread_step(2)
    hand_wait(1)
    ffn_part(1, 0, 1)
    b_send(1, 0, 1, 0)
    b_send(0, 2, 0, 2, range(PB // 2, PB))
    spread_step(3)
    ffn_part(1, 1, 1)
    b_send(1, 1, 0, 1)
    ffn_part(1, 2, 1)
    ffn_part(1, 3, 1)
    spread_step(4)

    ho = x

    def a_sum(pos, pc):
        part = pl.ds(pc * XR, XR)
        xacopy(pos, pc).wait_recv()
        pa[ho, pos, part] = pa[ho, pos, part] + xar[pos, part].astype(F32)

    def a_pos(way):
        return jnp.where(way == x, 2, 1)

    for pc in range(PX):
        part = pl.ds(pc * XR, XR)
        a_sum(0, pc)
        for way in (0, 1):
            as_[way, 0, part] = pa[ho, 0, part, way * H:(way + 1) * H].astype(BF)
            acopy(way, 0, pc).start()
    b_send(1, 2, 1, 2)
    spread_step(5)
    for pc in range(PX):
        part = pl.ds(pc * XR, XR)
        a_sum(1, pc)
        a_sum(2, pc)
        for way in (0, 1):
            as_[way, 1, part] = pa[ho, a_pos(way), part, (1 - way) * H:(2 - way) * H].astype(BF)
            acopy(way, 1, pc).start()
    def order(i):
        return (2 * (1 - core) + i) % PB if PB == 4 else i

    def b_join(hf, hx, pc):
        part = pl.ds(pl.multiple_of(pc * BR, BR), BR)
        bcopy(hx, 2, pc).wait_recv()
        bcopy(1 - hx, 1, pc).wait_recv()
        return pb[hf, 3, part] + br[hx, 2, part].astype(F32) + br[1 - hx, 1, part].astype(F32)

    for pc in range(PX):
        part = pl.ds(pc * XR, XR)
        for way in (0, 1):
            acopy(way, 0, pc).wait_recv()
            as_[way, 2, part] = (pa[ho, a_pos(way), part, way * H:(way + 1) * H]
                                 + ar[way, 0, part].astype(F32)).astype(BF)
            acopy(way, 2, pc).start()

    for i in range(PB):
        pc = order(i)
        part = pl.ds(pl.multiple_of(pc * BR, BR), BR)
        xbs[part] = b_join(1 - ho, 1 - x, pc).astype(BF)
        xbcopy(pc).start()

    for pc in range(PX):
        part = pl.ds(pc * XR, XR)
        a_sum(3, pc)
        for way in (0, 1):
            acopy(way, 1, pc).wait_recv()
            acopy(way, 2, pc).wait_recv()
        for h in (0, 1):
            pa[ho, 3, part, h * H:(h + 1) * H] = (pa[ho, 3, part, h * H:(h + 1) * H]
                                                  + ar[h, 2, part].astype(F32) + ar[1 - h, 1, part].astype(F32))

    give_rows = pl.multiple_of((1 - core) * rows, rows)
    keep_rows = pl.multiple_of(core * rows, rows)

    def pcopy(i):
        c = (slice(0, CA), slice(CA, FFN))[i]
        return remote(ps.at[:, c], pr.at[:, c], pss.at[i], prs.at[i], mate)

    ps[:, :CA] = pa[ho, 3, pl.ds(give_rows, rows), :]
    pcopy(0).start()
    for i in range(PB):
        pc = order(i)
        part = pl.ds(pl.multiple_of(pc * BR, BR), BR)
        pb[ho, 3, part] = b_join(ho, x, pc)
    for i in range(PB):
        pc = order(i)
        part = pl.ds(pl.multiple_of(pc * BR, BR), BR)
        xbcopy(pc).wait_recv()
        pb[ho, 3, part] = pb[ho, 3, part] + xbr[part].astype(F32)
        if i == PB // 2 - 1:
            ps[:, CA:] = pb[ho, 3, pl.ds(give_rows, rows), :]
            pcopy(1).start()

    inv = lax.rsqrt(fin[:, :1] / (gate.shape[0] * N) + EPSILON)

    def finish(i, own, c0, c1):
        pcopy(i).wait_recv()
        other = pr[:, c0:c1] * inv
        own = own * inv
        g = jnp.where(core == 0, own, other)
        u = jnp.where(core == 0, other, own)
        hid[:, c0:c1] = g / (1.0 + jnp.exp(-g)) * u

    finish(0, pa[ho, 3, pl.ds(keep_rows, rows), :], 0, CA)
    finish(1, pb[ho, 3, pl.ds(keep_rows, rows), :], CA, FFN)

    @pl.loop(1, N)
    def _(i):
        exchange(tb, tr, t_s, t_r, i).wait_send()
        exchange(qs, qr, q_s, q_r, i).wait_send()

    for i in range(8):
        remote(att.at[s], att.at[s], c_s.at[i], c_r.at[i], mate).wait_send()
        for r in (0, 1):
            ref = mgf.at[core, t]
            remote(ref, ref, mt_s.at[r, i], mt_r.at[r, i], mate).wait_send()
    res_copy().wait_send()
    for i in range(chips):
        egive(i).wait_send()
        if i:
            ecopy(i).wait_send()
    for pc in range(PA):
        xcopy(pc).wait_send()
        for way in (0, 1):
            ycopy(way, 0, pc).wait_send()
            ycopy(way, 1, pc).wait_send()
            ylast(way, pc).wait_send()
    for way in (0, 1):
        for pc in range(PP):
            pair_copy(way, pc).wait_send()
        for r in (0, 1):
            for pc in range(PZ[r]):
                for k in range(4):
                    if k > 0 or way == r:
                        rs(way, k, r, pc).wait_send()
                    if k < 3 or way == r:
                        ag(way, k, r, pc).wait_send()
        for m in range(3):
            for pc in range(PB):
                bcopy(way, m, pc).wait_send()
            for pc in range(PX):
                acopy(way, m, pc).wait_send()
    for pc in range(PB):
        xbcopy(pc).wait_send()
    for k in range(4):
        for pc in range(PX):
            xacopy(k, pc).wait_send()
    for i in (0, 1):
        pcopy(i).wait_send()
    for c in (0, 1):
        @pl.when(core == c)
        def _():
            w_far(c).wait_send()

    @pl.when(diag)
    def _():
        fin_pair().wait_send()

    @pl.when(on_right)
    def _():
        fin_copy(0).wait_send()

    @pl.when(on_left)
    def _():
        fin_copy(1).wait_send()

    @pl.when(off_diag)
    def _():
        sq_copy((s - t + N) % N).wait_send()


def body(
    queries,
    kv_pool,
    block_table,
    cached_lengths,
    arrivals,
    arrival_section,
    arrival_row,
    out_weight,
    residual,
    norm_gain,
    gate_weight,
    up_weight,
):
    rows, heads, hd = queries.shape
    width, ffn = gate_weight.shape
    m = CAP * heads
    entries = arrival_section.shape[0]
    cb = ffn - CA
    vm = pl.BlockSpec(memory_space=pltpu.VMEM)
    hbm = pl.BlockSpec(memory_space=pl.ANY)
    sm = pl.BlockSpec(memory_space=pltpu.SMEM)
    dma = pltpu.SemaphoreType.DMA

    def v(*shape, dtype=BF):
        return pltpu.VMEM(shape, dtype)

    scratch = [
        v(*kv_pool.shape[1:]), v(*arrivals.shape[1:]),
        v(N, m, 128), v(N, m, 128),
        v(N, m, hd), v(N, m, hd),
        v(N, 2 * heads * entries, hd), v(N, 2 * heads * entries, hd, dtype=F32),
        v(rows * heads, hd, dtype=F32),
        v(N, rows, heads * hd + 128), v(*out_weight.shape),
        v(N * entries, heads * hd), v(N * entries, heads * hd),
        v(N * entries, width), v(N * entries, width), v(8, N * entries, dtype=F32),
        v(8, 2, rows, width, dtype=F32), v(2, 4, 2, rows, width), v(2, 4, 2, rows, width),
        v(2, rows, width), v(2, rows, width), v(rows, width), v(2, N, rows, width), v(2, width, ffn),
        v(2, 4, 2 * rows, cb, dtype=F32), v(2, 4, 2 * rows, CA, dtype=F32),
        v(2, 3, 2 * rows, cb), v(2, 3, 2 * rows, cb),
        v(2, 3, 2 * rows, CA // 2), v(2, 3, 2 * rows, CA // 2),
        v(4, 2 * rows, CA), v(4, 2 * rows, CA),
        v(2 * rows, cb), v(2 * rows, cb),
        v(rows, ffn, dtype=F32), v(rows, ffn, dtype=F32),
        v(rows, 128, dtype=F32), v(N, rows, 128, dtype=F32), v(rows, 128, dtype=F32),
        dma((4,)), dma((N,)), dma((N,)), dma((N,)), dma((N,)),
        dma((N // 2,)), dma((N // 2,)), dma((N // 2,)), dma((N // 2,)),
        dma((2, 4, PA)), dma((2, 4, PA)), dma((8,)), dma((8,)),
        dma((2, 4, 2, 4)), dma((2, 4, 2, 4)), dma((2, PP)), dma((2, PP)), dma((2, 4, 2, 4)), dma((2, 4, 2, 4)), dma, dma,
        dma((2, 8)), dma((2, 8)),
        dma, dma, dma((2, 3, PB)), dma((2, 3, PB)), dma((2, 3, PX)), dma((2, 3, PX)),
        dma((4, PX)), dma((4, PX)), dma((PB,)), dma((PB,)), dma((2,)), dma((2,)),
        dma, dma((N,)), dma((3,)), dma,
    ]
    return pl.pallas_call(
        layer_kernel,
        out_shape=(jax.ShapeDtypeStruct(residual.shape, F32), jax.ShapeDtypeStruct((rows, ffn), F32)),
        in_specs=[sm, sm, vm, vm, vm, hbm, hbm, hbm, vm, vm, hbm, hbm],
        out_specs=(vm, vm),
        scratch_shapes=scratch,
        compiler_params=pltpu.CompilerParams(
            collective_id=1, has_side_effects=True, vmem_limit_bytes=VMEM_LIMIT),
        name="layer",
    )(arrival_section, arrival_row, queries.reshape(rows * heads, hd), block_table.T, cached_lengths,
      kv_pool, arrivals, out_weight, residual, norm_gain, gate_weight, up_weight)


def solution(mesh):
    placed = (
        P("section", "tensor", None),
        P(None, "section", None, None),
        P("section", None),
        P("section"),
        P(None, "section", None, None),
        P("section"),
        P("section"),
        P("tensor", "section"),
        P("tensor", "section"),
        P("section"),
        P("section", "tensor"),
        P("section", "tensor"),
    )
    return jax.shard_map(
        body,
        mesh=mesh,
        in_specs=placed,
        out_specs=(P("tensor", "section"), P("section", "tensor")),
        check_vma=False,
    )
```

```python
import jax
import jax.numpy as jnp
from jax import lax
from jax.experimental import pallas as pl
from jax.experimental.pallas import tpu as pltpu
from jax.sharding import PartitionSpec as P

MESH = pl.DeviceIdType.MESH
CAP = 2
NEG_LARGE = -1e30
EPSILON = 1e-05
VMEM_LIMIT = 60 * 1024 * 1024
BF = jnp.bfloat16
F32 = jnp.float32
N = 16
CA = 768
PZ = (4, 2)
PP = 2
PA = 2
PB = 4
PX = 4


def section_of(x, y, core):
    return x * 8 + y * 2 + core


def remote(src, dst, ssem, rsem, dev):
    return pltpu.make_async_remote_copy(
        src_ref=src, dst_ref=dst, send_sem=ssem, recv_sem=rsem,
        device_id=dev, device_id_type=MESH)


def signal(sem, dev):
    pl.semaphore_signal(sem, inc=1, device_id=dev, device_id_type=MESH)


def layer_kernel(sec, row, q, tab, lens, pool, arr, wo_in, res, gain, gate, up,
                 proj_out, hid,
                 kvp, kva, tb, tr, qs, qr, eb, ef, acc, att, wo, dh, dl, dwh, dwl, idr,
                 pz, rbuf, sbuf, xs, xr, resx, mgf, wf,
                 pb, pa, bs, br, as_, ar, xas, xar, xbs, xbr, ps, pr, sq, sqr, fin,
                 l_sem, t_s, t_r, q_s, q_r, e_s, e_r, eg_s, eg_r, y_s, y_r, c_s, c_r,
                 rs_s, rs_r, px_s, px_r, ag_s, ag_r, rx_s, rx_r, mt_s, mt_r,
                 w_s, w_r, bss, brs, ass, ars, xass, xars, xbss, xbrs, pss, prs,
                 sqs, sqrs, dgs, dgr):
    s, t = lax.axis_index("section"), lax.axis_index("tensor")
    x, y, core = s // 8, (s // 2) % 4, s % 2
    xh, z = t // 8, t % 8
    diag = s == t
    off_diag = jnp.logical_not(diag)
    mate = (section_of(x, y, 1 - core), t)
    xpeer = (section_of(1 - x, y, core), t)
    hpeer = (s, (1 - xh) * 8 + z)

    def ydev(way):
        return (section_of(x, (y + 1 + 2 * way) % 4, core), t)

    def zdev(way):
        return (s, xh * 8 + (z + 1 + 6 * way) % 8)

    barrier = pltpu.get_barrier_semaphore()

    @pl.loop(1, N)
    def _(i):
        signal(barrier, ((s + i) % N, t))

    for dev in (zdev(0), zdev(1), hpeer):
        signal(barrier, dev)

    pool_copy = pltpu.make_async_copy(pool.at[t // 2], kvp, l_sem.at[0])
    arr_copy = pltpu.make_async_copy(arr.at[t // 2], kva, l_sem.at[1])
    wo_copy = pltpu.make_async_copy(wo_in, wo, l_sem.at[2])

    def w_own(c):
        return pltpu.make_async_copy(gate if c == 0 else up, wf.at[c], l_sem.at[3])

    def w_far(c):
        return remote(up if c == 0 else gate, wf.at[c], w_s, w_r, mate)

    pool_copy.start()
    arr_copy.start()
    wo_copy.start()

    HD = q.shape[1]
    rows = res.shape[0]
    heads = q.shape[0] // rows
    M = CAP * heads
    i2 = lax.broadcasted_iota(jnp.int32, (N * M, 128), 0)
    slot = i2 // heads
    head = i2 % heads
    secs = [sec[e] for e in range(sec.shape[0])]
    targets = []
    for e, d in enumerate(secs):
        rank = sum([(secs[p] == d).astype(jnp.int32) for p in range(e)], jnp.int32(0))
        targets.append(d * CAP + rank)
    ids = jnp.full((N * M, 128), -1, jnp.int32)
    for e, target in enumerate(targets):
        ids = jnp.where(slot == target, row[e], ids)
    tb[...] = ids.astype(F32).astype(BF).reshape(N, M, 128)

    def exchange(src, dst, ss, rs, i):
        d = (s + i) % N
        return remote(src.at[d], dst.at[s], ss.at[i], rs.at[i], (d, t))

    def start_all(src, dst, ss, rs):
        @pl.loop(1, N)
        def _(i):
            exchange(src, dst, ss, rs, i).start()

    def wait_all(src, dst, ss, rs):
        @pl.loop(1, N)
        def _(i):
            exchange(src, dst, ss, rs, i).wait_recv()

    pl.semaphore_wait(barrier, N - 1 + 3)

    start_all(tb, tr, t_s, t_r)
    tr[s] = tb[s]

    def res_copy():
        return remote(res, resx, rx_s, rx_r, hpeer)

    res_copy().start()
    for c in (0, 1):
        @pl.when(core == c)
        def _():
            w_own(c).start()
            w_far(c).start()

    blocks = kvp.shape[0]
    len_row = lens[...].reshape(1, rows)
    which = lax.broadcasted_iota(jnp.int32, (2 * blocks, rows), 0)
    limits = jnp.zeros((2 * blocks, rows), jnp.int32)
    for b in range(blocks):
        limit = jnp.zeros((1, rows), jnp.int32)
        for j in range(tab.shape[0]):
            limit = jnp.maximum(limit, jnp.where(tab[j:j + 1, :] == b, len_row - j * 128, 0))
        limits = jnp.where(which == b, limit // 2, jnp.where(which == blocks + b, limit % 2, limits))
    def spread_of(shape, axis):
        return (lax.broadcasted_iota(jnp.int32, shape, axis) // heads
                == lax.broadcasted_iota(jnp.int32, shape, 1 - axis)).astype(F32).astype(BF)

    spread = spread_of((rows * heads, rows), 0)
    limits = lax.dot_general(spread, limits.astype(F32).astype(BF), (((1,), (1,)), ((), ())),
                             preferred_element_type=F32)
    lane = lax.broadcasted_iota(jnp.int32, (rows * heads, 128), 1).astype(F32)
    ok = [lane < 2.0 * limits[:, b:b + 1] + limits[:, blocks + b:blocks + b + 1] for b in range(blocks)]
    pool_copy.wait()
    kv = kvp[...].reshape(-1, 2 * HD)
    scale_qk = HD ** -0.5

    def scores(a, k):
        return lax.dot_general(a, k, (((1,), (1,)), ((), ())), preferred_element_type=F32) * scale_qk

    okc = jnp.concatenate([o.astype(F32) for o in ok], axis=1) > 0.5
    sc = jnp.where(okc, scores(q[...], kv[:, :HD]), NEG_LARGE)
    m_p = jnp.max(sc, axis=1, keepdims=True)
    p = jnp.where(okc, jnp.exp(sc - m_p), 0.0)
    l_p = jnp.sum(p, axis=1, keepdims=True)
    acc[...] = jnp.dot(p.astype(BF), kv[:, HD:], preferred_element_type=F32) / l_p
    for h in range(heads):
        att[s, :, h * HD:(h + 1) * HD] = acc[pl.ds(h, rows, stride=heads), :].astype(BF)

    def terms(v):
        hi = v.astype(BF).astype(F32)
        mid = (v - hi).astype(BF).astype(F32)
        return hi, mid, v - hi - mid

    lane_i = lax.broadcasted_iota(jnp.int32, (rows * heads, 128), 1)
    row_i = lax.broadcasted_iota(jnp.int32, (rows * heads, 128), 0)
    stats = jnp.zeros((rows * heads, 128), F32)
    for i, term in enumerate(terms(m_p) + terms(l_p)):
        stats = jnp.where(lane_i // heads == i, term, stats)
    stats = jnp.where(lane_i % heads == row_i % heads, stats, 0.0)
    att[s, :, heads * HD:] = jnp.dot(spread_of((rows, rows * heads), 1), stats.astype(BF),
                                     preferred_element_type=F32).astype(BF)

    def rows_of(ref, blk, pc, pieces):
        step = rows // pieces
        return ref.at[blk, pl.ds(pc * step, step)]

    def ycopy(way, h, pc):
        ref = rows_of(att, section_of(x if h == 0 else 1 - x, y, core), pc, PA)
        return remote(ref, ref, y_s.at[way, h, pc], y_r.at[way, h, pc], ydev(way))

    def ylast(way, pc):
        ref = rows_of(att, section_of(way, (y + 3 - 2 * way) % 4, core), pc, PA)
        return remote(ref, ref, y_s.at[way, 2, pc], y_r.at[way, 2, pc], ydev(way))

    def xcopy(pc):
        ref = rows_of(att, s, pc, PA)
        return remote(ref, ref, y_s.at[0, 3, pc], y_r.at[0, 3, pc], xpeer)

    def give(i, blk):
        remote(att.at[blk], att.at[blk], c_s.at[i], c_r.at[i], mate).start()

    for pc in range(PA):
        xcopy(pc).start()
        for way in (0, 1):
            ycopy(way, 0, pc).start()
    give(0, s)

    wait_all(tb, tr, t_s, t_r)
    asked = tr[...].reshape(N * M, 128).astype(F32)
    ids = jnp.where(asked < 0.0, -1.0, asked * heads + head.astype(F32))
    lane2 = lax.broadcasted_iota(jnp.int32, (N * M, 128), 1)
    pick = jnp.concatenate([(ids == (lane2 + 128 * c).astype(F32)).astype(F32) for c in range(q.shape[0] // 128)], axis=1)
    qs[...] = jnp.dot(pick.astype(BF), q[...], preferred_element_type=F32).astype(BF).reshape(N, M, HD)
    start_all(qs, qr, q_s, q_r)
    qr[s] = qs[s]

    for pc in range(PA):
        xcopy(pc).wait_recv()
        for way in (0, 1):
            ycopy(way, 1, pc).start()
        ycopy(x, 0, pc).wait_recv()
        ylast(x, pc).start()
    give(1, section_of(1 - x, y, core))

    E = len(targets)
    HE = heads * E
    arr_copy.wait()
    kvn = kva[...].reshape(-1, 2 * HD)
    slot_of = lax.broadcasted_iota(jnp.int32, (HE, N * M), 0)
    want = jnp.zeros((HE, N * M), jnp.int32)
    for e, target in enumerate(targets):
        want = jnp.where(slot_of % E == e, target * heads + slot_of // E, want)
    sel = (want == lax.broadcasted_iota(jnp.int32, (HE, N * M), 1)).astype(F32).astype(BF)
    ok_n = (lax.broadcasted_iota(jnp.int32, (HE, E * 128), 1) // 128
            == lax.broadcasted_iota(jnp.int32, (HE, E * 128), 0) % E)
    lane_e = lax.broadcasted_iota(jnp.int32, (HE, 128), 1)
    entry = lax.broadcasted_iota(jnp.int32, (HE, 128), 0) % E
    place = jnp.zeros((HE, 128), jnp.int32)
    for e in range(E):
        place = jnp.where(entry == e, jnp.where(lane_e == 6, secs[e], row[e]), place)
    wait_all(qs, qr, q_s, q_r)
    qn = jnp.dot(sel, qr[...].reshape(N * M, HD), preferred_element_type=F32).astype(BF)
    sn = jnp.where(ok_n, scores(qn, kvn[:, :HD]), NEG_LARGE)
    m_n = jnp.max(sn, axis=1, keepdims=True)
    pn = jnp.where(ok_n, jnp.exp(sn - m_n), 0.0)
    l_n = jnp.sum(pn, axis=1, keepdims=True)
    eb[s, :HE] = jnp.dot(pn.astype(BF), kvn[:, HD:], preferred_element_type=F32).astype(BF)
    tile = place.astype(F32)
    for i, term in enumerate(terms(m_n) + terms(l_n)):
        tile = jnp.where(lane_e == i, term, tile)
    eb[s, HE:] = tile.astype(BF)

    chips = N // 2
    chip = s // 2

    def ecopy(i):
        return remote(eb.at[s], eb.at[s], e_s.at[i], e_r.at[i], (((chip + i) % chips) * 2 + core, t))

    def egive(i):
        src = ((chip + chips - i) % chips) * 2 + core
        return remote(eb.at[src], eb.at[src], eg_s.at[i], eg_r.at[i], mate)

    for i in range(1, chips):
        ecopy(i).start()
    egive(0).start()

    for pc in range(PA):
        ycopy(1 - x, 0, pc).wait_recv()
    for way in (0, 1):
        give(2 + way, section_of(x, (y + 3 - 2 * way) % 4, core))
    for pc in range(PA):
        ycopy(1 - x, 1, pc).wait_recv()
        ylast(1 - x, pc).start()
    for pc in range(PA):
        ycopy(x, 1, pc).wait_recv()
    for way in (0, 1):
        give(4 + way, section_of(1 - x, (y + 3 - 2 * way) % 4, core))
    for way in (x, 1 - x):
        for pc in range(PA):
            ylast(way, pc).wait_recv()
        give(6 + way, section_of(way, (y + 2) % 4, core))
    for i in range(1, chips):
        ecopy(i).wait_recv()
        egive(i).start()
    wo_copy.wait()
    for i in range(8):
        remote(att.at[s], att.at[s], c_s.at[i], c_r.at[i], mate).wait_recv()

    def project(slot_, off):
        zz = (z + off) % 8
        a = jnp.concatenate([att[zz, :, :heads * HD], att[8 + zz, :, :heads * HD]], 0)
        v = jnp.dot(a, wo[...], preferred_element_type=F32)
        pz[slot_, 0] = v[:rows]
        pz[slot_, 1] = v[rows:]

    def off_of(slot_):
        k = (slot_ + 1) // 2
        return jnp.where(slot_ % 2 == 1, 4 - k, 4 + k) % 8

    def cut(r, pc):
        step = rows // PZ[r]
        return pl.ds(pc * step, step)

    def rs(way, k, r, pc):
        part = cut(r, pc)
        return remote(sbuf.at[way, k, r, part], rbuf.at[way, k, r, part],
                      rs_s.at[way, k, r, pc], rs_r.at[way, k, r, pc], zdev(way))

    def rs_send(way, k, r, add):
        for pc in range(PZ[r]):
            part = cut(r, pc)
            v = pz[0 if k == 0 else 2 * k - 1 + way, r, part]
            if add:
                rs(way, k - 1, r, pc).wait_recv()
                v = v + rbuf[way, k - 1, r, part].astype(F32)
            sbuf[way, k, r, part] = v.astype(BF)
            rs(way, k, r, pc).start()

    @pl.loop(0, 8)
    def _(i):
        project(i, off_of(i))

    for i in range(chips):
        egive(i).wait_recv()
    ef[...] = eb[...].astype(F32)
    NE = N * E
    eye = lax.broadcasted_iota(jnp.int32, (NE, NE), 0) == lax.broadcasted_iota(jnp.int32, (NE, NE), 1)
    before = lax.broadcasted_iota(jnp.int32, (NE, NE), 1) < lax.broadcasted_iota(jnp.int32, (NE, NE), 0)

    def across(col):
        return jnp.sum(jnp.where(eye, col, 0.0), axis=0, keepdims=True)

    def three(v, i, step):
        return v[:, i:i + 1] + v[:, i + step:i + step + 1] + v[:, i + 2 * step:i + 2 * step + 1]

    info = ef[:, pl.ds(HE, E), :].reshape(NE, 128)
    id_col = info[:, 6:7] * rows + info[:, 7:8]
    id_row = across(id_col)
    idr[...] = jnp.broadcast_to(id_row, idr.shape)
    same = id_col == id_row
    first = jnp.sum(jnp.where(jnp.logical_and(same, before), 1.0, 0.0), axis=1, keepdims=True) < 0.5
    pick_rows = (id_col == lax.broadcasted_iota(jnp.int32, (NE, N * rows), 1).astype(F32)).astype(F32).astype(BF)
    old = jnp.dot(pick_rows, att[...].reshape(N * rows, -1), preferred_element_type=F32)
    old_stats = old[:, heads * HD:]
    for h in range(heads):
        info = ef[:, pl.ds(HE + h * E, E), :].reshape(NE, 128)
        m_row = across(three(info, 0, 1))
        l_row = across(three(info, 3, 1))
        m_old = three(old_stats, h, heads)
        l_old = three(old_stats, 3 * heads + h, heads)
        logit = jnp.where(same, m_row, NEG_LARGE)
        top = jnp.maximum(m_old, jnp.max(logit, axis=1, keepdims=True))
        w = jnp.where(same, jnp.exp(logit - top), 0.0)
        kept = jnp.exp(m_old - top) * l_old
        total = kept + jnp.sum(w * l_row, axis=1, keepdims=True)
        old_h = old[:, h * HD:(h + 1) * HD]
        new = ef[:, pl.ds(h * E, E), :].reshape(NE, HD).astype(BF)
        joined = (kept * old_h + jnp.dot(w.astype(BF), new, preferred_element_type=F32)) / total
        diff = jnp.where(first, joined - old_h, 0.0)
        hi = diff.astype(BF)
        dh[:, h * HD:(h + 1) * HD] = hi
        dl[:, h * HD:(h + 1) * HD] = (diff - hi.astype(F32)).astype(BF)
    diff = (jnp.dot(dh[...], wo[...], preferred_element_type=F32)
            + jnp.dot(dl[...], wo[...], preferred_element_type=F32))
    dwh[...] = diff.astype(BF)
    dwl[...] = (diff - dwh[...].astype(F32)).astype(BF)

    def correct(slot_, off):
        zz = (z + off) % 8
        at = lax.broadcasted_iota(jnp.int32, (2 * rows, NE), 0)
        at = (at + zz * rows + jnp.where(at >= rows, 7 * rows, 0)).astype(F32)
        put = (at == idr[0:1, :]).astype(F32).astype(BF)
        v = (jnp.dot(put, dwh[...], preferred_element_type=F32)
             + jnp.dot(put, dwl[...], preferred_element_type=F32))
        pz[slot_, 0] = pz[slot_, 0] + v[:rows]
        pz[slot_, 1] = pz[slot_, 1] + v[rows:]

    correct(0, 4)
    for r in (0, 1):
        rs_send(r, 0, r, False)

    @pl.loop(1, 3)
    def _(i):
        correct(i, off_of(i))

    for r in (0, 1):
        rs_send(1 - r, 1, r, False)

    @pl.loop(3, 8)
    def _(i):
        correct(i, off_of(i))

    for k in (1, 2, 3):
        for r in (0, 1):
            rs_send(r, k, r, True)
            if k > 1:
                rs_send(1 - r, k, r, True)

    PR = rows // PP

    def pair_copy(r, pc):
        part = pl.ds(pc * PR, PR)
        return remote(xs.at[r, part], xr.at[r, part], px_s.at[r, pc], px_r.at[r, pc], hpeer)

    for r in (0, 1):
        for pc in range(PZ[r]):
            part = cut(r, pc)
            for way in (0, 1):
                rs(way, 3, r, pc).wait_recv()
            v = pz[7, r, part] + rbuf[0, 3, r, part].astype(F32) + rbuf[1, 3, r, part].astype(F32)
            pz[7, r, part] = v
            xs[r, part] = v.astype(BF)
            if (pc + 1) % (PZ[r] // PP) == 0:
                pair_copy(r, pc // (PZ[r] // PP)).start()

    def blk_of(way, k, r):
        return r * 8 + (z + 8 + (2 * way - 1) * k) % 8

    def ag(way, k, r, pc):
        ref = mgf.at[core, blk_of(way, k, r), cut(r, pc)]
        return remote(ref, ref, ag_s.at[way, k, r, pc], ag_r.at[way, k, r, pc], zdev(way))

    def hand(r, i, blk):
        ref = mgf.at[core, blk]
        remote(ref, ref, mt_s.at[r, i], mt_r.at[r, i], mate).start()

    def hand_wait(r):
        for i in range(8):
            ref = mgf.at[core, t]
            remote(ref, ref, mt_s.at[r, i], mt_r.at[r, i], mate).wait_recv()

    def ag_step(k, r):
        for pc in range(PZ[r]):
            for way in (0, 1):
                ag(way, k - 1, r, pc).wait_recv()
                if k < 3 or way == r:
                    ag(way, k, r, pc).start()
        for way in (0, 1):
            hand(r, 2 * (k - 1) + 1 + way, blk_of(way, k, r))

    def ag_end(r):
        for pc in range(PZ[r]):
            ag(r, 3, r, pc).wait_recv()
        hand(r, 7, blk_of(0, 4, r))

    def ag_begin(r):
        for pp in range(PP):
            part = pl.ds(pp * PR, PR)
            pair_copy(r, pp).wait_recv()
            proj = pz[7, r, part] + xr[r, part].astype(F32)
            mixed = proj + jnp.where(xh == r, res[part].astype(F32), resx[part].astype(F32))
            mgf[core, blk_of(0, 0, r), part] = (mixed * gain[...].reshape(1, -1).astype(F32)).astype(BF)
            for pc in range(pp * PZ[r] // PP, (pp + 1) * PZ[r] // PP):
                for way in (0, 1):
                    ag(way, 0, r, pc).start()

            @pl.when(xh == r)
            def _():
                proj_out[part] = proj
                sq[part] = jnp.sum(mixed * mixed, axis=1, keepdims=True) + jnp.zeros((PR, sq.shape[1]), F32)
        hand(r, 0, blk_of(0, 0, r))

    def sq_copy(i):
        return remote(sq, sqr.at[i], sqs, sqrs.at[i], (t, t))

    def fin_copy(way):
        return remote(fin, fin, dgs.at[way], dgr, zdev(way))

    def fin_pair():
        return remote(fin, fin, dgs.at[2], dgr, hpeer)

    dz = (z + 8 - s % 8) % 8
    hops = jnp.where(dz <= 4, dz, 8 - dz) + jnp.where(xh == s // 8, 0, 1)
    on_right = dz <= 3
    on_left = jnp.logical_or(dz == 0, dz >= 6)

    def spread_step(p):
        @pl.when(hops == p)
        def _():
            if p == 0:
                total_sq = sq[...]
                for i in range(1, N):
                    sq_copy(i).wait_recv()
                    total_sq = total_sq + sqr[i]
                fin[...] = total_sq
                fin_pair().start()
            else:
                fin_copy(0).wait_recv()

            @pl.when(on_right)
            def _():
                fin_copy(0).start()

            @pl.when(on_left)
            def _():
                fin_copy(1).start()

    res_copy().wait_recv()
    ag_begin(0)
    ag_step(1, 0)
    ag_begin(1)

    @pl.when(off_diag)
    def _():
        sq_copy((s - t + N) % N).start()

    ag_step(2, 0)
    ag_step(1, 1)
    ag_step(3, 0)
    ag_step(2, 1)
    ag_end(0)
    spread_step(0)

    R = 2 * rows
    FFN = gate.shape[1]
    CB = FFN - CA
    H = CA // 2
    BR = R // PB
    XR = R // PX
    for c in (0, 1):
        @pl.when(core == c)
        def _():
            w_own(c).wait()
            w_far(c).wait_recv()

    def yoff(k):
        return (y + jnp.where(k == 0, 2, jnp.where(k == 1, 1, jnp.where(k == 2, 3, 0)))) % 4

    def ffn_part(hf, pos, hx):
        k = (0, 2 - hx, 1 + hx, 3)[pos]
        b = hx * 8 + 2 * yoff(k)
        a0 = mgf[0, pl.ds(b, 2)].reshape(R, -1)
        a1 = mgf[1, pl.ds(b, 2)].reshape(R, -1)

        def cols(c0, c1):
            return (jnp.dot(a0, wf[0, :, c0:c1], preferred_element_type=F32)
                    + jnp.dot(a1, wf[1, :, c0:c1], preferred_element_type=F32))

        pb[hf, pos] = cols(CA, FFN)
        pa[hf, pos] = cols(0, CA)

        @pl.when(hx != x)
        def _():
            for pc in range(PX):
                part = pl.ds(pc * XR, XR)
                xas[pos, part] = pa[hf, pos, part].astype(BF)
                xacopy(pos, pc).start()

    def bcopy(way, m, pc):
        part = pl.ds(pc * BR, BR)
        return remote(bs.at[way, m, part], br.at[way, m, part], bss.at[way, m, pc], brs.at[way, m, pc], ydev(way))

    def acopy(way, m, pc):
        part = pl.ds(pc * XR, XR)
        return remote(as_.at[way, m, part], ar.at[way, m, part], ass.at[way, m, pc], ars.at[way, m, pc], ydev(way))

    def xacopy(k, pc):
        part = pl.ds(pc * XR, XR)
        return remote(xas.at[k, part], xar.at[k, part], xass.at[k, pc], xars.at[k, pc], xpeer)

    def xbcopy(pc):
        part = pl.ds(pl.multiple_of(pc * BR, BR), BR)
        return remote(xbs.at[part], xbr.at[part], xbss.at[pc], xbrs.at[pc], xpeer)

    def b_send(hf, pos, way, m, pieces=range(PB)):
        for pc in pieces:
            part = pl.ds(pc * BR, BR)
            v = pb[hf, pos, part]
            if m == 2:
                bcopy(way, 0, pc).wait_recv()
                v = v + br[way, 0, part].astype(F32)
            bs[way, m, part] = v.astype(BF)
            bcopy(way, m, pc).start()

    hand_wait(0)
    ffn_part(0, 0, 0)
    b_send(0, 0, 0, 0)
    ag_step(3, 1)
    ffn_part(0, 1, 0)
    b_send(0, 1, 1, 1)
    spread_step(1)
    ag_end(1)
    ffn_part(0, 2, 0)
    ffn_part(0, 3, 0)
    b_send(0, 2, 0, 2, range(PB // 2))
    spread_step(2)
    hand_wait(1)
    ffn_part(1, 0, 1)
    b_send(1, 0, 1, 0)
    b_send(0, 2, 0, 2, range(PB // 2, PB))
    spread_step(3)
    ffn_part(1, 1, 1)
    b_send(1, 1, 0, 1)
    ffn_part(1, 2, 1)
    ffn_part(1, 3, 1)
    spread_step(4)

    ho = x

    def a_sum(pos, pc):
        part = pl.ds(pc * XR, XR)
        xacopy(pos, pc).wait_recv()
        pa[ho, pos, part] = pa[ho, pos, part] + xar[pos, part].astype(F32)

    def a_pos(way):
        return jnp.where(way == x, 2, 1)

    for pc in range(PX):
        part = pl.ds(pc * XR, XR)
        a_sum(0, pc)
        for way in (0, 1):
            as_[way, 0, part] = pa[ho, 0, part, way * H:(way + 1) * H].astype(BF)
            acopy(way, 0, pc).start()
    b_send(1, 2, 1, 2)
    spread_step(5)
    for pc in range(PX):
        part = pl.ds(pc * XR, XR)
        a_sum(1, pc)
        a_sum(2, pc)
        for way in (0, 1):
            as_[way, 1, part] = pa[ho, a_pos(way), part, (1 - way) * H:(2 - way) * H].astype(BF)
            acopy(way, 1, pc).start()
    def order(i):
        return (2 * (1 - core) + i) % PB if PB == 4 else i

    def b_join(hf, hx, pc):
        part = pl.ds(pl.multiple_of(pc * BR, BR), BR)
        bcopy(hx, 2, pc).wait_recv()
        bcopy(1 - hx, 1, pc).wait_recv()
        return pb[hf, 3, part] + br[hx, 2, part].astype(F32) + br[1 - hx, 1, part].astype(F32)

    for pc in range(PX):
        part = pl.ds(pc * XR, XR)
        for way in (0, 1):
            acopy(way, 0, pc).wait_recv()
            as_[way, 2, part] = (pa[ho, a_pos(way), part, way * H:(way + 1) * H]
                                 + ar[way, 0, part].astype(F32)).astype(BF)
            acopy(way, 2, pc).start()

    for i in range(PB):
        pc = order(i)
        part = pl.ds(pl.multiple_of(pc * BR, BR), BR)
        xbs[part] = b_join(1 - ho, 1 - x, pc).astype(BF)
        xbcopy(pc).start()

    for pc in range(PX):
        part = pl.ds(pc * XR, XR)
        a_sum(3, pc)
        for way in (0, 1):
            acopy(way, 1, pc).wait_recv()
            acopy(way, 2, pc).wait_recv()
        for h in (0, 1):
            pa[ho, 3, part, h * H:(h + 1) * H] = (pa[ho, 3, part, h * H:(h + 1) * H]
                                                  + ar[h, 2, part].astype(F32) + ar[1 - h, 1, part].astype(F32))

    give_rows = pl.multiple_of((1 - core) * rows, rows)
    keep_rows = pl.multiple_of(core * rows, rows)

    def pcopy(i):
        c = (slice(0, CA), slice(CA, FFN))[i]
        return remote(ps.at[:, c], pr.at[:, c], pss.at[i], prs.at[i], mate)

    ps[:, :CA] = pa[ho, 3, pl.ds(give_rows, rows), :]
    pcopy(0).start()
    for i in range(PB):
        pc = order(i)
        part = pl.ds(pl.multiple_of(pc * BR, BR), BR)
        pb[ho, 3, part] = b_join(ho, x, pc)
    for i in range(PB):
        pc = order(i)
        part = pl.ds(pl.multiple_of(pc * BR, BR), BR)
        xbcopy(pc).wait_recv()
        pb[ho, 3, part] = pb[ho, 3, part] + xbr[part].astype(F32)
        if i == PB // 2 - 1:
            ps[:, CA:] = pb[ho, 3, pl.ds(give_rows, rows), :]
            pcopy(1).start()

    inv = lax.rsqrt(fin[:, :1] / (gate.shape[0] * N) + EPSILON)

    def finish(i, own, c0, c1):
        pcopy(i).wait_recv()
        other = pr[:, c0:c1] * inv
        own = own * inv
        g = jnp.where(core == 0, own, other)
        u = jnp.where(core == 0, other, own)
        hid[:, c0:c1] = g / (1.0 + jnp.exp(-g)) * u

    finish(0, pa[ho, 3, pl.ds(keep_rows, rows), :], 0, CA)
    finish(1, pb[ho, 3, pl.ds(keep_rows, rows), :], CA, FFN)

    @pl.loop(1, N)
    def _(i):
        exchange(tb, tr, t_s, t_r, i).wait_send()
        exchange(qs, qr, q_s, q_r, i).wait_send()

    for i in range(8):
        remote(att.at[s], att.at[s], c_s.at[i], c_r.at[i], mate).wait_send()
        for r in (0, 1):
            ref = mgf.at[core, t]
            remote(ref, ref, mt_s.at[r, i], mt_r.at[r, i], mate).wait_send()
    res_copy().wait_send()
    for i in range(chips):
        egive(i).wait_send()
        if i:
            ecopy(i).wait_send()
    for pc in range(PA):
        xcopy(pc).wait_send()
        for way in (0, 1):
            ycopy(way, 0, pc).wait_send()
            ycopy(way, 1, pc).wait_send()
            ylast(way, pc).wait_send()
    for way in (0, 1):
        for pc in range(PP):
            pair_copy(way, pc).wait_send()
        for r in (0, 1):
            for pc in range(PZ[r]):
                for k in range(4):
                    if k > 0 or way == r:
                        rs(way, k, r, pc).wait_send()
                    if k < 3 or way == r:
                        ag(way, k, r, pc).wait_send()
        for m in range(3):
            for pc in range(PB):
                bcopy(way, m, pc).wait_send()
            for pc in range(PX):
                acopy(way, m, pc).wait_send()
    for pc in range(PB):
        xbcopy(pc).wait_send()
    for k in range(4):
        for pc in range(PX):
            xacopy(k, pc).wait_send()
    for i in (0, 1):
        pcopy(i).wait_send()
    for c in (0, 1):
        @pl.when(core == c)
        def _():
            w_far(c).wait_send()

    @pl.when(diag)
    def _():
        fin_pair().wait_send()

    @pl.when(on_right)
    def _():
        fin_copy(0).wait_send()

    @pl.when(on_left)
    def _():
        fin_copy(1).wait_send()

    @pl.when(off_diag)
    def _():
        sq_copy((s - t + N) % N).wait_send()


def body(
    queries,
    kv_pool,
    block_table,
    cached_lengths,
    arrivals,
    arrival_section,
    arrival_row,
    out_weight,
    residual,
    norm_gain,
    gate_weight,
    up_weight,
):
    rows, heads, hd = queries.shape
    width, ffn = gate_weight.shape
    m = CAP * heads
    entries = arrival_section.shape[0]
    cb = ffn - CA
    vm = pl.BlockSpec(memory_space=pltpu.VMEM)
    hbm = pl.BlockSpec(memory_space=pl.ANY)
    sm = pl.BlockSpec(memory_space=pltpu.SMEM)
    dma = pltpu.SemaphoreType.DMA

    def v(*shape, dtype=BF):
        return pltpu.VMEM(shape, dtype)

    scratch = [
        v(*kv_pool.shape[1:]), v(*arrivals.shape[1:]),
        v(N, m, 128), v(N, m, 128),
        v(N, m, hd), v(N, m, hd),
        v(N, 2 * heads * entries, hd), v(N, 2 * heads * entries, hd, dtype=F32),
        v(rows * heads, hd, dtype=F32),
        v(N, rows, heads * hd + 128), v(*out_weight.shape),
        v(N * entries, heads * hd), v(N * entries, heads * hd),
        v(N * entries, width), v(N * entries, width), v(8, N * entries, dtype=F32),
        v(8, 2, rows, width, dtype=F32), v(2, 4, 2, rows, width), v(2, 4, 2, rows, width),
        v(2, rows, width), v(2, rows, width), v(rows, width), v(2, N, rows, width), v(2, width, ffn),
        v(2, 4, 2 * rows, cb, dtype=F32), v(2, 4, 2 * rows, CA, dtype=F32),
        v(2, 3, 2 * rows, cb), v(2, 3, 2 * rows, cb),
        v(2, 3, 2 * rows, CA // 2), v(2, 3, 2 * rows, CA // 2),
        v(4, 2 * rows, CA), v(4, 2 * rows, CA),
        v(2 * rows, cb), v(2 * rows, cb),
        v(rows, ffn, dtype=F32), v(rows, ffn, dtype=F32),
        v(rows, 128, dtype=F32), v(N, rows, 128, dtype=F32), v(rows, 128, dtype=F32),
        dma((4,)), dma((N,)), dma((N,)), dma((N,)), dma((N,)),
        dma((N // 2,)), dma((N // 2,)), dma((N // 2,)), dma((N // 2,)),
        dma((2, 4, PA)), dma((2, 4, PA)), dma((8,)), dma((8,)),
        dma((2, 4, 2, 4)), dma((2, 4, 2, 4)), dma((2, PP)), dma((2, PP)), dma((2, 4, 2, 4)), dma((2, 4, 2, 4)), dma, dma,
        dma((2, 8)), dma((2, 8)),
        dma, dma, dma((2, 3, PB)), dma((2, 3, PB)), dma((2, 3, PX)), dma((2, 3, PX)),
        dma((4, PX)), dma((4, PX)), dma((PB,)), dma((PB,)), dma((2,)), dma((2,)),
        dma, dma((N,)), dma((3,)), dma,
    ]
    return pl.pallas_call(
        layer_kernel,
        out_shape=(jax.ShapeDtypeStruct(residual.shape, F32), jax.ShapeDtypeStruct((rows, ffn), F32)),
        in_specs=[sm, sm, vm, vm, vm, hbm, hbm, hbm, vm, vm, hbm, hbm],
        out_specs=(vm, vm),
        scratch_shapes=scratch,
        compiler_params=pltpu.CompilerParams(
            collective_id=1, has_side_effects=True, vmem_limit_bytes=VMEM_LIMIT),
        name="layer",
    )(arrival_section, arrival_row, queries.reshape(rows * heads, hd), block_table.T, cached_lengths,
      kv_pool, arrivals, out_weight, residual, norm_gain, gate_weight, up_weight)


def solution(mesh):
    placed = (
        P("section", "tensor", None),
        P(None, "section", None, None),
        P("section", None),
        P("section"),
        P(None, "section", None, None),
        P("section"),
        P("section"),
        P("tensor", "section"),
        P("tensor", "section"),
        P("section"),
        P("section", "tensor"),
        P("section", "tensor"),
    )
    return jax.shard_map(
        body,
        mesh=mesh,
        in_specs=placed,
        out_specs=(P("tensor", "section"), P("section", "tensor")),
        check_vma=False,
    )
```
